128 devices in a mesh: node: 32 (over z, y, core), local: 4 (over x).
Axes of the slice: x: 4, y: 4, z: 4, core: 2. Of those that a mesh axis runs over, the one named last changes fastest.
Arguments:
- tokens: bfloat16 [16384, 7168], P(('node', 'local')), may hold values from -6 to 6
- node_set: int32 [16384, 2], P(('node', 'local')), may hold values from 0 to 31, all different within a row; in each aligned block of 128 rows (0 to 127, 128 to 255, ...) at most 12 rows name the same one
- gate_weights: float32 [16384, 2], P(('node', 'local')), may hold values from 0.2 to 1
- w_gate: bfloat16 [32, 7168, 1024], P('node', 'local'), may hold values from -0.0625 to 0.0625
- w_up: bfloat16 [32, 7168, 1024], P('node', 'local'), may hold values from -0.0625 to 0.0625
- w_down: bfloat16 [32, 1024, 7168], P('node', None, 'local'), may hold values from -0.1875 to 0.1875
Outputs:
- mixed: bfloat16 [16384, 7168], P(('node', 'local'))
The draws below stay inside these ranges and needn't reach their ends.
Inputs may be any that keep to these rules, and one draw needn't show every extreme that they name: `node_set`: each row names 2 different experts; among the rows of one device no expert is named by more than 12 rows, and in every draw some expert is named by exactly 12 rows of some device.
All inputs are finite; a program needn't handle non-finite values.
Results may differ from the reference program's by a relative error of at most 0.0058.
Values may be sent and summed in bfloat16 or wider, within the bound.
A program may use at most 128 MiB of HBM per device.

```python
import math
import jax
import jax.numpy as jnp
import numpy as np
from jax import lax

D = 7168
FF = 1024
ROUTES = 2
TOK_DEV = 128
EXPERTS = 32
CAP = 12
TOKENS = 16384
N_NODE = 32
N_LOCAL = 4


def block_levels(stream_key, extent, shards, smallest, high):
    gain, own = 1.0, jax.random.fold_in(stream_key, 6)
    for axis_at, shards_of in shards:
        draws = jnp.exp(jax.random.uniform(jax.random.fold_in(own, axis_at), (shards_of,), jnp.float32, smallest / len(shards), high / len(shards)))
        gain = gain * jnp.repeat(draws, extent[axis_at] // shards_of).reshape([-1 if axis == axis_at else 1 for axis in range(len(extent))])
    return gain


def shared_out(own_key, own, number, rows, count, top, most, slope):
    ranking = jax.random.permutation(own_key, count)
    crowded, common = shares(count, rows * top, most, slope, True), shares(count, rows * top, most, slope, False)
    places = jnp.arange(count)

    def named(lengths, turn):
        used = int((lengths > 0).sum())
        fixed = max(1, used // 4)
        shifted = fixed + (places - fixed + turn * (used - fixed)) % max(1, count - fixed)
        return jnp.zeros((count,), jnp.int32).at[ranking[jnp.where(places < fixed, places, shifted)]].set(jnp.asarray(lengths, jnp.int32))

    lengths = jnp.where(number % 4 == 0, named(crowded, number // 4), named(common, number - number // 4 - 1))
    mixed = jax.random.permutation(jax.random.fold_in(own, 3), count)
    source_of, taker = mixed[0:count // 2 * 2:2], mixed[1:count // 2 * 2:2]
    margin = jnp.minimum(lengths[source_of] - 1, most - lengths[taker]) // 2
    margin = jnp.where((source_of == ranking[0]) | (taker == ranking[0]) | (lengths[taker] == 0), 0, jnp.maximum(margin, 0))
    shifted = jax.random.randint(jax.random.fold_in(own, 4), (count // 2,), 0, 1 << 20) % (margin + 1)
    lengths = lengths.at[source_of].add(-shifted).at[taker].add(shifted)
    labels = jnp.searchsorted(jnp.cumsum(lengths), jnp.arange(rows * top), side="right").astype(jnp.int32)
    listing = labels.reshape(top, rows).T
    listing = listing[jax.random.permutation(jax.random.fold_in(own, 1), rows)]
    turn = jax.random.randint(jax.random.fold_in(own, 2), (rows, 1), 0, top)
    return jnp.take_along_axis(listing, (jnp.arange(top)[None, :] + turn) % top, axis=1)


def shares(count, total, limit, lean, full):
    portions = [(1 << 20) // math.isqrt(standing ** lean) + 1 for standing in range(1, count + 1)]
    largest = limit if full else min(limit, max(-(-total // count), total * portions[0] // sum(portions)))
    least = 1 if total - largest >= count - 1 else 0
    counts, spare = [largest] + [least] * (count - 1), total - largest - least * (count - 1)
    while spare > 0:
        movable = [i for i in range(1, count) if counts[i] < largest] or [i for i in range(1, count) if counts[i] < limit]
        whole, left = sum([portions[i] for i in movable]), spare
        for i in movable:
            addition = min(limit - counts[i], max(1, left * portions[i] // whole), spare)
            counts[i] = counts[i] + addition
            spare = spare - addition
    return np.array(counts)


def normal_values(stream_key, dims, deviation, reach, split=(), held_as=jnp.bfloat16):
    level = block_levels(stream_key, dims, split, -0.22, 0.18) if split else 1.0
    result = jax.random.normal(stream_key, dims, jnp.float32) * deviation * level
    return jnp.minimum(jnp.maximum(result, -reach), reach).astype(held_as)


def setup_inputs(seed: int = 0) -> dict:
    key_of = jax.random.split(jax.random.key(seed), 7)
    tokens = normal_values(key_of[0], (TOKENS, D), 1.0, 6.0, ((0, 128),))
    node_set_keys = jax.random.split(jax.random.fold_in(key_of[1], 1), TOKENS // TOK_DEV)
    node_set_turns = jax.random.permutation(jax.random.fold_in(key_of[1], 3), TOKENS // TOK_DEV)
    node_set = jax.vmap(lambda own, number: shared_out(jax.random.fold_in(key_of[1], 2), own, number, TOK_DEV, N_NODE, ROUTES, CAP, 2))(node_set_keys, node_set_turns).reshape((TOKENS, ROUTES))
    gate_weights = jnp.clip(jnp.exp(math.log(1.0) - 1.609438 * jax.random.uniform(key_of[2], (TOKENS, ROUTES), jnp.float32) ** block_levels(key_of[2], (TOKENS, ROUTES), ((0, 128),), -0.2, 0.2)), 0.2, 1.0)
    w_gate = normal_values(key_of[3], (EXPERTS, D, FF), D ** -0.5, 0.0625, ((0, 32), (1, 4)))
    w_up = normal_values(key_of[4], (EXPERTS, D, FF), D ** -0.5, 0.0625, ((0, 32), (1, 4)))
    w_down = normal_values(key_of[5], (EXPERTS, FF, D), FF ** -0.5, 0.1875, ((0, 32), (2, 4)))
    return {"tokens": tokens, "node_set": node_set, "gate_weights": gate_weights, "w_gate": w_gate, "w_up": w_up, "w_down": w_down}


def reference(tokens, node_set, gate_weights, w_gate, w_up, w_down):
    total_tokens = tokens.shape[0]
    most_rows = N_NODE * N_LOCAL * CAP

    def one_expert(carry, expert):
        chosen_mask = node_set == expert
        hit = jnp.any(chosen_mask, axis=1)
        weight_of = jnp.sum(jnp.where(chosen_mask, gate_weights, jnp.float32(0.0)), axis=1)
        rows_index = jnp.nonzero(hit, size=most_rows, fill_value=0)[0].astype(jnp.int32)
        valid = (jnp.arange(most_rows, dtype=jnp.int32) < jnp.sum(hit.astype(jnp.int32))).astype(jnp.float32)
        chosen = jnp.take(tokens, rows_index, axis=0)
        gate_mat = lax.dynamic_index_in_dim(w_gate, expert, 0, keepdims=False)
        up_mat = lax.dynamic_index_in_dim(w_up, expert, 0, keepdims=False)
        down_mat = lax.dynamic_index_in_dim(w_down, expert, 0, keepdims=False)
        pre_gate = jnp.dot(chosen, gate_mat, preferred_element_type=jnp.float32)
        pre_up = jnp.dot(chosen, up_mat, preferred_element_type=jnp.float32)
        hidden = (jax.nn.silu(pre_gate) * pre_up).astype(jnp.bfloat16)
        answer = jnp.dot(hidden, down_mat, preferred_element_type=jnp.float32).astype(jnp.bfloat16)
        scale_rows = jnp.take(weight_of, rows_index, axis=0) * valid
        carry = carry.at[rows_index].add(answer.astype(jnp.float32) * scale_rows[:, None])
        return carry, None

    start_sum = jnp.zeros((total_tokens, D), jnp.float32)
    total, unused = lax.scan(one_expert, start_sum, jnp.arange(EXPERTS, dtype=jnp.int32))
    return total.astype(jnp.bfloat16)
```

```python
import functools

import jax
import jax.numpy as jnp
from jax import lax
from jax.experimental import pallas as pl
from jax.experimental.pallas import tpu as pltpu
from jax.sharding import PartitionSpec as P

MESH = pl.DeviceIdType.MESH
F32 = jnp.float32
BF16 = jnp.bfloat16
CHIPS = (
    (0, 0), (1, 0), (3, 0), (0, 2),
    (3, 3), (1, 3), (3, 1), (2, 1),
    (1, 2), (3, 2), (2, 3), (2, 2),
    (0, 1), (0, 3), (2, 0), (1, 1),
)
OFFSETS = tuple((dz, dy, dc) for dz, dy in CHIPS for dc in range(2))
NODES, LOCALS = 32, 4
GROUPS = 4
PER = NODES // GROUPS


def kernel(tok_rows, quarter, ff, cap,
           meta_ref, tok_ref, wg_ref, wu_ref, wd_ref, out_ref,
           meta, xin, pick, sbuf, abuf, wgu, wd, pre, rsbuf, hid, rbuf, uhi, ulo, acc, mbuf,
           w_sem, l_sem, ms_sem, mr_sem, xs_sem, xr_sem, ds_sem, dr_sem, ps_sem, pr_sem, hs_sem, hr_sem,
           as_sem, ar_sem, fs_sem, fr_sem):
    slots = LOCALS * cap
    grows = PER * slots
    own = grows // LOCALS
    node, loc = lax.axis_index("node"), lax.axis_index("local")
    z, y, c = node // 8, (node // 2) % 4, node % 2

    def to(o):
        dz, dy, dc = OFFSETS[o]
        return (((z + dz) % 4) * 4 + (y + dy) % 4) * 2 + (c + dc) % 2

    def back(o):
        dz, dy, dc = OFFSETS[o]
        return (((z + 4 - dz) % 4) * 4 + (y + 4 - dy) % 4) * 2 + (c + dc) % 2

    def xto(d):
        return (loc + d) % LOCALS

    barrier = pltpu.get_barrier_semaphore()
    for o in range(1, NODES):
        pl.semaphore_signal(barrier, inc=1, device_id=(to(o), loc), device_id_type=MESH)
    for d in range(1, LOCALS):
        pl.semaphore_signal(barrier, inc=1, device_id=(node, xto(d)), device_id_type=MESH)

    def rows(ref, start, size):
        return ref.at[pl.ds(pl.multiple_of(start, 16), size)]

    def cols(j):
        return pl.ds(pl.multiple_of(j * quarter, 128), quarter)

    w_copies = [
        pltpu.make_async_copy(wg_ref.at[0], wgu.at[:, pl.ds(0, ff)], w_sem.at[0]),
        pltpu.make_async_copy(wu_ref.at[0], wgu.at[:, pl.ds(ff, ff)], w_sem.at[1]),
        pltpu.make_async_copy(wd_ref.at[0], wd, w_sem.at[2]),
    ]
    own_tok = pltpu.make_async_copy(tok_ref.at[:, cols(loc)], rows(xin, loc * tok_rows, tok_rows), l_sem.at[0])
    own_tok.start()
    pl.semaphore_wait(barrier, NODES - 1 + LOCALS - 1)

    def remote(src, dst, ss, rs, n, x):
        return pltpu.make_async_remote_copy(
            src_ref=src, dst_ref=dst, send_sem=ss, recv_sem=rs, device_id=(n, x), device_id_type=MESH)

    meta_copies, x_copies = [], []
    for d in (2, 1, 3):
        meta_copies.append(remote(meta_ref, meta.at[loc], ms_sem.at[d - 1], mr_sem.at[d - 1], node, xto(d)))
        meta_copies[-1].start()
    for d in (2, 1, 3):
        x_copies.append(remote(tok_ref.at[:, cols(xto(d))], rows(xin, loc * tok_rows, tok_rows),
                               xs_sem.at[d - 1], xr_sem.at[d - 1], node, xto(d)))
        x_copies[-1].start()
    for w in w_copies:
        w.start()
    meta[loc] = meta_ref[...]
    own_tok.wait()
    for m in meta_copies:
        m.wait()
    for m in x_copies:
        m.wait()

    d_copies = []
    for g in range(GROUPS):
        at = lax.broadcasted_iota(jnp.int32, (slots, tok_rows), 0)
        for i in range(PER):
            row_id = (at + to(g * PER + i) * slots).astype(F32)
            for b in range(LOCALS):
                d0 = meta[b, 0:1, :] + float(b * cap)
                d1 = meta[b, 1:2, :] + float(b * cap)
                hit = jnp.where(row_id == d0, 1.0, 0.0) + jnp.where(row_id == d1, 1.0, 0.0)
                pick[i * slots:(i + 1) * slots, b * tok_rows:(b + 1) * tok_rows] = hit.astype(BF16)

        @pl.loop(0, quarter // 256)
        def _(t):
            at = pl.ds(pl.multiple_of(t * 256, 256), 256)
            sbuf[g * grows:(g + 1) * grows, at] = jnp.dot(
                pick[...], xin[:, at], preferred_element_type=F32).astype(BF16)

        for o in range(g * PER, (g + 1) * PER):
            src, dst = sbuf.at[pl.ds(o * slots, slots)], abuf.at[pl.ds(o * slots, slots)]
            if o == 0:
                d_copies.append(pltpu.make_async_copy(src, dst, l_sem.at[1]))
            else:
                d_copies.append(remote(src, dst, ds_sem.at[o], dr_sem.at[o], to(o), loc))
            d_copies[-1].start()

    p_copies, h_copies, a_copies = {}, {}, {}

    def stage_a(g):
        for o in range(g * PER, (g + 1) * PER):
            d_copies[o].wait() if o == 0 else d_copies[o].wait_recv()
        if g == 0:
            w_copies[0].wait()
            w_copies[1].wait()

        @pl.loop(0, 2 * ff // 256)
        def _(t):
            at = pl.ds(pl.multiple_of(t * 256, 256), 256)
            pre[g * grows:(g + 1) * grows, at] = jnp.dot(
                abuf[g * grows:(g + 1) * grows, :], wgu[:, at], preferred_element_type=F32).astype(BF16)

        for d in (2, 1, 3):
            p_copies[g, d] = remote(rows(pre, g * grows + xto(d) * own, own), rsbuf.at[g, d - 1],
                                    ps_sem.at[g, d - 1], pr_sem.at[g, d - 1], node, xto(d))
            p_copies[g, d].start()

    def stage_b(g):
        for d in (2, 1, 3):
            p_copies[g, d].wait_recv()
        mine = pl.ds(pl.multiple_of(g * grows + loc * own, 16), own)

        @pl.loop(0, ff // 256)
        def _(t):
            at_g = pl.ds(pl.multiple_of(t * 256, 256), 256)
            at_u = pl.ds(pl.multiple_of(t * 256 + ff, 256), 256)
            gate, up = pre[mine, at_g].astype(F32), pre[mine, at_u].astype(F32)
            for d in range(3):
                gate = gate + rsbuf[g, d, :, at_g].astype(F32)
                up = up + rsbuf[g, d, :, at_u].astype(F32)
            hid[mine, at_g] = (gate / (1.0 + jnp.exp(-gate)) * up).astype(BF16)

        for d in (2, 1, 3):
            h_copies[g, d] = remote(hid.at[mine], hid.at[mine], hs_sem.at[g, d - 1], hr_sem.at[g, d - 1],
                                    node, xto(d))
            h_copies[g, d].start()

    def stage_c(g):
        for d in (2, 1, 3):
            h_copies[g, d].wait_recv()
        if g == 0:
            w_copies[2].wait()

        @pl.loop(0, quarter // 256)
        def _(t):
            at = pl.ds(pl.multiple_of(t * 256, 256), 256)
            abuf[g * grows:(g + 1) * grows, at] = jnp.dot(
                hid[g * grows:(g + 1) * grows, :], wd[:, at], preferred_element_type=F32).astype(BF16)

        for o in range(g * PER, (g + 1) * PER):
            src, dst = abuf.at[pl.ds(o * slots, slots)], rbuf.at[pl.ds(o * slots, slots)]
            if o == 0:
                a_copies[o] = pltpu.make_async_copy(src, dst, l_sem.at[2])
            else:
                a_copies[o] = remote(src, dst, as_sem.at[o], ar_sem.at[o], back(o), loc)
            a_copies[o].start()

    def mix_weights(g):
        spot = lax.broadcasted_iota(jnp.int32, (tok_rows, grows), 1)
        slot_id = spot + (to(g * PER) - 0) * slots
        for i in range(1, PER):
            slot_id = jnp.where(spot >= i * slots, spot + (to(g * PER + i) - i) * slots, slot_id)
        slot_id = slot_id.astype(F32)
        for b in range(LOCALS):
            m = jnp.transpose(meta[b])
            d0, d1 = m[:, 0:1] + float(b * cap), m[:, 1:2] + float(b * cap)
            w = jnp.where(slot_id == d0, m[:, 2:3], 0.0) + jnp.where(slot_id == d1, m[:, 3:4], 0.0)
            high = w.astype(BF16)
            uhi[b * tok_rows:(b + 1) * tok_rows, :] = high
            ulo[b * tok_rows:(b + 1) * tok_rows, :] = (w - high.astype(F32)).astype(BF16)

    def stage_m(g):
        mix_weights(g)
        for o in range(g * PER, (g + 1) * PER):
            a_copies[o].wait() if o == 0 else a_copies[o].wait_recv()

        @pl.loop(0, quarter // 256)
        def _(t):
            at = pl.ds(pl.multiple_of(t * 256, 256), 256)
            got = rbuf[g * grows:(g + 1) * grows, at]
            part = jnp.dot(uhi[...], got, preferred_element_type=F32) + jnp.dot(
                ulo[...], got, preferred_element_type=F32)
            if g > 0:
                part = part + acc[:, at]
            if g < GROUPS - 1:
                acc[:, at] = part
            else:
                mbuf[:, at] = part.astype(BF16)

    for step in range(GROUPS + 2):
        if step < GROUPS:
            stage_a(step)
        if 1 <= step <= GROUPS:
            stage_b(step - 1)
        if step >= 2:
            stage_c(step - 2)
    for g in range(GROUPS):
        stage_m(g)

    f_copies = []
    for d in (2, 1, 3):
        f_copies.append(remote(rows(mbuf, xto(d) * tok_rows, tok_rows), out_ref.at[:, cols(loc)],
                               fs_sem.at[d - 1], fr_sem.at[d - 1], node, xto(d)))
        f_copies[-1].start()
    own_out = pltpu.make_async_copy(rows(mbuf, loc * tok_rows, tok_rows), out_ref.at[:, cols(loc)], l_sem.at[3])
    own_out.start()
    for o in range(1, NODES):
        d_copies[o].wait_send()
        a_copies[o].wait_send()
    for g in range(GROUPS):
        for d in (1, 2, 3):
            p_copies[g, d].wait_send()
            h_copies[g, d].wait_send()
    own_out.wait()
    for f in f_copies:
        f.wait()


def shards(tokens, node_set, gate_weights, w_gate, w_up, w_down):
    tok_rows, width = tokens.shape
    quarter = width // LOCALS
    ff = w_gate.shape[2]
    routes = node_set.shape[1]
    cap = 3 * tok_rows * routes // (2 * NODES)
    slots = LOCALS * cap
    total = NODES * slots
    grows = total // GROUPS
    own = grows // LOCALS

    member = node_set[:, :, None] == jnp.arange(NODES, dtype=jnp.int32)[None, None, :]
    counts = jnp.sum(member.astype(F32), axis=1)
    earlier = jnp.tri(tok_rows, k=-1, dtype=BF16)
    before = jnp.dot(earlier, counts.astype(BF16), preferred_element_type=F32)
    slot = jnp.sum(jnp.where(member, before[:, None, :], 0.0), axis=2)
    dest = (node_set * slots).astype(F32) + slot
    meta = jnp.concatenate([dest.T, gate_weights.T, jnp.zeros((4, tok_rows), F32)], axis=0)

    any_spec = pl.BlockSpec(memory_space=pl.ANY)
    dma = pltpu.SemaphoreType.DMA
    return pl.pallas_call(
        functools.partial(kernel, tok_rows, quarter, ff, cap),
        name="routed_experts",
        out_shape=jax.ShapeDtypeStruct((tok_rows, width), BF16),
        in_specs=[pl.BlockSpec(memory_space=pltpu.VMEM)] + [any_spec] * 4,
        out_specs=any_spec,
        scratch_shapes=[
            pltpu.VMEM((LOCALS, 8, tok_rows), F32),
            pltpu.VMEM((LOCALS * tok_rows, quarter), BF16),
            pltpu.VMEM((grows, LOCALS * tok_rows), BF16),
            pltpu.VMEM((total, quarter), BF16),
            pltpu.VMEM((total, quarter), BF16),
            pltpu.VMEM((quarter, 2 * ff), BF16),
            pltpu.VMEM((ff, quarter), BF16),
            pltpu.VMEM((total, 2 * ff), BF16),
            pltpu.VMEM((GROUPS, LOCALS - 1, own, 2 * ff), BF16),
            pltpu.VMEM((total, ff), BF16),
            pltpu.VMEM((total, quarter), BF16),
            pltpu.VMEM((LOCALS * tok_rows, grows), BF16),
            pltpu.VMEM((LOCALS * tok_rows, grows), BF16),
            pltpu.VMEM((LOCALS * tok_rows, quarter), F32),
            pltpu.VMEM((LOCALS * tok_rows, quarter), BF16),
            dma((3,)), dma((4,)), dma((3,)), dma((3,)), dma((3,)), dma((3,)),
            dma((NODES,)), dma((NODES,)),
            dma((GROUPS, 3)), dma((GROUPS, 3)), dma((GROUPS, 3)), dma((GROUPS, 3)),
            dma((NODES,)), dma((NODES,)), dma((3,)), dma((3,)),
        ],
        compiler_params=pltpu.CompilerParams(
            collective_id=0, has_side_effects=True, vmem_limit_bytes=60 * 2**20),
        cost_estimate=pl.CostEstimate(flops=20 * 10**9, bytes_accessed=15 * 10**6, transcendentals=10**6),
    )(meta, tokens, w_gate, w_up, w_down)


def solution(mesh):
    placed = (
        P(("node", "local"), None),
        P(("node", "local"), None),
        P(("node", "local"), None),
        P("node", "local", None),
        P("node", "local", None),
        P("node", None, "local"),
    )
    return jax.shard_map(
        shards, mesh=mesh, in_specs=placed, out_specs=P(("node", "local"), None), check_vma=False
    )
```

```python
import functools

import jax
import jax.numpy as jnp
from jax import lax
from jax.experimental import pallas as pl
from jax.experimental.pallas import tpu as pltpu
from jax.sharding import PartitionSpec as P

MESH = pl.DeviceIdType.MESH
F32 = jnp.float32
BF16 = jnp.bfloat16
NODES, LOCALS = 32, 4
STEPS = ((0, 0), (0, 1), (2, 0), (2, 1), (1, 0), (1, 1), (3, 0), (3, 1))
PLANES = (0, 3, 1, 2)
HALVES = 2
PER = len(STEPS) // HALVES
GROUPS = len(PLANES) * HALVES


def kernel(tok_rows, quarter, ff, cap,
           meta_ref, tok_ref, wg_ref, wu_ref, wd_ref, out_ref,
           meta, zin, pick, sbuf, abuf, wgu, wd, pre, part, ownf, rsbuf, hid, rbuf, uhi, ulo, acc, mbuf,
           w_sem, l_sem, ms_sem, mr_sem, ns_sem, nr_sem, xs_sem, xr_sem, zs_sem, zr_sem, os_sem, or_sem,
           ds_sem, dr_sem, ps_sem, pr_sem, hs_sem, hr_sem, as_sem, ar_sem, fs_sem, fr_sem):
    slots = LOCALS * cap
    prows = len(STEPS) * slots
    grows = PER * slots
    own = grows // LOCALS
    ptok = LOCALS * tok_rows
    node, loc = lax.axis_index("node"), lax.axis_index("local")
    z, y, c = node // 8, (node // 2) % 4, node % 2

    def at_node(dz, dy, dc):
        return (((z + dz) % 4) * 4 + (y + dy) % 4) * 2 + (c + dc) % 2

    def back(r, i):
        dy, dc = STEPS[i]
        return at_node(PLANES[r], 4 - dy, dc)

    def expert(r, i):
        dy, dc = STEPS[i]
        return at_node(4 - PLANES[r], dy, dc)

    def xto(d):
        return (loc + d) % LOCALS

    def rows(ref, start, size):
        return ref.at[pl.ds(pl.multiple_of(start, 16), size)]

    def cols(j):
        return pl.ds(pl.multiple_of(j * quarter, 128), quarter)

    def tile(t, base=0):
        return pl.ds(pl.multiple_of(t * 256 + base, 256), 256)

    def remote(src, dst, ss, rs, n, x):
        return pltpu.make_async_remote_copy(
            src_ref=src, dst_ref=dst, send_sem=ss, recv_sem=rs, device_id=(n, x), device_id_type=MESH)

    barrier = pltpu.get_barrier_semaphore()
    for r in range(len(PLANES)):
        for i in range(len(STEPS)):
            if (r, i) != (0, 0):
                pl.semaphore_signal(barrier, inc=1, device_id=(back(r, i), loc), device_id_type=MESH)
    for d in range(1, LOCALS):
        pl.semaphore_signal(barrier, inc=1, device_id=(node, xto(d)), device_id_type=MESH)
    own_tok = pltpu.make_async_copy(tok_ref.at[:, cols(loc)], rows(zin, loc * tok_rows, tok_rows), l_sem.at[0])
    own_tok.start()
    pl.semaphore_wait(barrier, NODES - 1 + LOCALS - 1)

    m_copies, n_copies, x_copies, z_copies, o_copies = {}, {}, {}, {}, {}
    for d in (1, 3, 2):
        m_copies[d] = remote(meta_ref, meta.at[0, loc], ms_sem.at[d - 1], mr_sem.at[d - 1], node, xto(d))
        m_copies[d].start()

    def z_send(d, src):
        at = ((loc + LOCALS - d) % LOCALS) * tok_rows
        for r, dz in ((1, 1), (2, 3)):
            z_copies[r, d] = remote(src, rows(zin, r * ptok + at, tok_rows), zs_sem.at[r - 1, d], zr_sem.at[r - 1, d],
                                    at_node(dz, 0, 0), loc)
            z_copies[r, d].start()

    def z_forward(d):
        half = tok_rows // 2
        at = ((loc + LOCALS - d) % LOCALS) * tok_rows
        for r, dz, shift in ((1, 1, 0), (2, 3, half)):
            z_copies[r, d].wait_recv()
            o_copies[r, d] = remote(rows(zin, r * ptok + at + shift, half), rows(zin, 3 * ptok + at + shift, half),
                                    os_sem.at[r - 1, d], or_sem.at[r - 1, d], at_node(dz, 0, 0), loc)
            o_copies[r, d].start()

    for d in (1, 3, 2):
        x_copies[d] = remote(tok_ref.at[:, cols(xto(d))], rows(zin, loc * tok_rows, tok_rows),
                             xs_sem.at[d - 1], xr_sem.at[d - 1], node, xto(d))
        x_copies[d].start()
    z_send(0, tok_ref.at[:, cols(loc)])
    w_copies = [
        pltpu.make_async_copy(wg_ref.at[0], wgu.at[:, pl.ds(0, ff)], w_sem.at[0]),
        pltpu.make_async_copy(wu_ref.at[0], wgu.at[:, pl.ds(ff, ff)], w_sem.at[1]),
        pltpu.make_async_copy(wd_ref.at[0], wd, w_sem.at[2]),
    ]
    meta[0, loc] = meta_ref[...]
    for d in (1, 3, 2):
        m_copies[d].wait()
    for r, dz in ((1, 1), (2, 3), (3, 2)):
        n_copies[r] = remote(meta.at[0], meta.at[r], ns_sem.at[r - 1], nr_sem.at[r - 1], at_node(dz, 0, 0), loc)
        n_copies[r].start()
    for w in w_copies:
        w.start()
    for d in (1, 3, 2):
        x_copies[d].wait_recv()
        z_send(d, rows(zin, ((loc + LOCALS - d) % LOCALS) * tok_rows, tok_rows))
    own_tok.wait()

    d_copies, p_copies, h_copies, a_copies = {}, {}, {}, {}

    def plane_send(r):
        if r > 0:
            n_copies[r].wait_recv()
        if r == 3:
            for d in (0, 1, 3, 2):
                o_copies[1, d].wait_recv()
                o_copies[2, d].wait_recv()
        at = lax.broadcasted_iota(jnp.int32, (slots, tok_rows), 0)
        for i in range(len(STEPS)):
            row_id = (at + at_node(0, *STEPS[i]) * slots).astype(F32)
            for b in range(LOCALS):
                d0 = meta[r, b, 0:1, :] + float(b * cap)
                d1 = meta[r, b, 1:2, :] + float(b * cap)
                hit = jnp.where(row_id == d0, 1.0, 0.0) + jnp.where(row_id == d1, 1.0, 0.0)
                pick[i * slots:(i + 1) * slots, b * tok_rows:(b + 1) * tok_rows] = hit.astype(BF16)

        @pl.loop(0, quarter // 256)
        def _(t):
            got = jnp.dot(pick[...], zin[r * ptok:(r + 1) * ptok, tile(t)], preferred_element_type=F32).astype(BF16)
            abuf[r * prows:r * prows + slots, tile(t)] = got[:slots]
            sbuf[r * prows + slots:(r + 1) * prows, tile(t)] = got[slots:]

        for i in range(1, len(STEPS)):
            at = pl.ds(r * prows + i * slots, slots)
            d_copies[r, i] = remote(sbuf.at[at], abuf.at[at], ds_sem.at[r, i], dr_sem.at[r, i],
                                    at_node(0, *STEPS[i]), loc)
            d_copies[r, i].start()

    def members(g):
        return [(g // HALVES, g % HALVES * PER + j) for j in range(PER)]

    def stage_a(g):
        for r, i in members(g):
            if i > 0:
                d_copies[r, i].wait_recv()
        if g == 0:
            w_copies[0].wait()
            w_copies[1].wait()

        @pl.loop(0, 2 * ff // 256)
        def _(t):
            part[...] = jnp.dot(abuf[g * grows:(g + 1) * grows, :], wgu[:, tile(t)], preferred_element_type=F32)
            pre[g * grows:(g + 1) * grows, tile(t)] = part[...].astype(BF16)
            ownf[g, :, tile(t)] = part[pl.ds(pl.multiple_of(loc * own, 16), own), :]

        for d in (2, 1, 3):
            p_copies[g, d] = remote(rows(pre, g * grows + xto(d) * own, own), rsbuf.at[g, d - 1],
                                    ps_sem.at[g, d - 1], pr_sem.at[g, d - 1], node, xto(d))
            p_copies[g, d].start()

    def stage_b(g):
        for d in (2, 1, 3):
            p_copies[g, d].wait_recv()
        mine = pl.ds(pl.multiple_of(g * grows + loc * own, 16), own)

        @pl.loop(0, ff // 256)
        def _(t):
            gate, up = ownf[g, :, tile(t)], ownf[g, :, tile(t, ff)]
            for d in range(3):
                gate = gate + rsbuf[g, d, :, tile(t)].astype(F32)
                up = up + rsbuf[g, d, :, tile(t, ff)].astype(F32)
            hid[mine, tile(t)] = (gate / (1.0 + jnp.exp(-gate)) * up).astype(BF16)

        for d in (2, 1, 3):
            h_copies[g, d] = remote(hid.at[mine], hid.at[mine], hs_sem.at[g, d - 1], hr_sem.at[g, d - 1],
                                    node, xto(d))
            h_copies[g, d].start()

    def stage_c(g):
        for d in (2, 1, 3):
            h_copies[g, d].wait_recv()
        if g == 0:
            w_copies[2].wait()

        @pl.loop(0, quarter // 256)
        def _(t):
            got = jnp.dot(hid[g * grows:(g + 1) * grows, :], wd[:, tile(t)],
                          preferred_element_type=F32).astype(BF16)
            if g == 0:
                rbuf[0:slots, tile(t)] = got[:slots]
                abuf[slots:grows, tile(t)] = got[slots:]
            else:
                abuf[g * grows:(g + 1) * grows, tile(t)] = got

        for r, i in members(g):
            if (r, i) != (0, 0):
                at = pl.ds(r * prows + i * slots, slots)
                a_copies[r, i] = remote(abuf.at[at], rbuf.at[at], as_sem.at[r, i], ar_sem.at[r, i], back(r, i), loc)
                a_copies[r, i].start()

    def stage_m(r):
        spot = lax.broadcasted_iota(jnp.int32, (tok_rows, prows), 1)
        slot_id = spot + expert(r, 0) * slots
        for i in range(1, len(STEPS)):
            slot_id = jnp.where(spot >= i * slots, spot + (expert(r, i) - i) * slots, slot_id)
        slot_id = slot_id.astype(F32)
        for b in range(LOCALS):
            m = jnp.transpose(meta[0, b])
            d0, d1 = m[:, 0:1] + float(b * cap), m[:, 1:2] + float(b * cap)
            w = jnp.where(slot_id == d0, m[:, 2:3], 0.0) + jnp.where(slot_id == d1, m[:, 3:4], 0.0)
            high = w.astype(BF16)
            uhi[b * tok_rows:(b + 1) * tok_rows, :] = high
            ulo[b * tok_rows:(b + 1) * tok_rows, :] = (w - high.astype(F32)).astype(BF16)
        for i in range(len(STEPS)):
            if (r, i) != (0, 0):
                a_copies[r, i].wait_recv()

        @pl.loop(0, quarter // 256)
        def _(t):
            got = rbuf[r * prows:(r + 1) * prows, tile(t)]
            mix = jnp.dot(uhi[...], got, preferred_element_type=F32) + jnp.dot(
                ulo[...], got, preferred_element_type=F32)
            if r > 0:
                mix = mix + acc[:, tile(t)]
            if r < len(PLANES) - 1:
                acc[:, tile(t)] = mix
            else:
                mbuf[:, tile(t)] = mix.astype(BF16)

    plane_send(0)
    z_forward(0)
    z_forward(1)
    z_forward(3)
    stage_a(0)
    stage_a(1)
    z_forward(2)
    plane_send(1)
    plane_send(2)
    stage_b(0)
    stage_b(1)
    stage_a(2)
    stage_c(0)
    stage_a(3)
    stage_c(1)
    plane_send(3)
    stage_b(2)
    stage_a(4)
    stage_b(3)
    stage_c(2)
    stage_a(5)
    stage_b(4)
    stage_c(3)
    stage_a(6)
    stage_b(5)
    stage_c(4)
    stage_a(7)
    stage_b(6)
    stage_c(5)
    stage_m(0)
    stage_b(7)
    stage_c(6)
    stage_c(7)
    stage_m(1)
    stage_m(2)
    stage_m(3)

    f_copies = []
    for d in (2, 1, 3):
        f_copies.append(remote(rows(mbuf, xto(d) * tok_rows, tok_rows), out_ref.at[:, cols(loc)],
                               fs_sem.at[d - 1], fr_sem.at[d - 1], node, xto(d)))
        f_copies[-1].start()
    own_out = pltpu.make_async_copy(rows(mbuf, loc * tok_rows, tok_rows), out_ref.at[:, cols(loc)], l_sem.at[1])
    own_out.start()
    for sent in (x_copies, n_copies, z_copies, o_copies, d_copies, a_copies, p_copies, h_copies):
        for copy in sent.values():
            copy.wait_send()
    own_out.wait()
    for f in f_copies:
        f.wait()


def shards(tokens, node_set, gate_weights, w_gate, w_up, w_down):
    tok_rows, width = tokens.shape
    quarter = width // LOCALS
    ff = w_gate.shape[2]
    routes = node_set.shape[1]
    cap = 3 * tok_rows * routes // (2 * NODES)
    slots = LOCALS * cap
    total = NODES * slots
    prows = len(STEPS) * slots
    grows = PER * slots
    own = grows // LOCALS

    member = node_set[:, :, None] == jnp.arange(NODES, dtype=jnp.int32)[None, None, :]
    counts = jnp.sum(member.astype(F32), axis=1)
    earlier = jnp.tri(tok_rows, k=-1, dtype=BF16)
    before = jnp.dot(earlier, counts.astype(BF16), preferred_element_type=F32)
    slot = jnp.sum(jnp.where(member, before[:, None, :], 0.0), axis=2)
    dest = (node_set * slots).astype(F32) + slot
    meta = jnp.concatenate([dest.T, gate_weights.T, jnp.zeros((4, tok_rows), F32)], axis=0)

    any_spec = pl.BlockSpec(memory_space=pl.ANY)
    dma = pltpu.SemaphoreType.DMA
    return pl.pallas_call(
        functools.partial(kernel, tok_rows, quarter, ff, cap),
        name="routed_experts",
        out_shape=jax.ShapeDtypeStruct((tok_rows, width), BF16),
        in_specs=[pl.BlockSpec(memory_space=pltpu.VMEM)] + [any_spec] * 4,
        out_specs=any_spec,
        scratch_shapes=[
            pltpu.VMEM((len(PLANES), LOCALS, 8, tok_rows), F32),
            pltpu.VMEM((len(PLANES) * LOCALS * tok_rows, quarter), BF16),
            pltpu.VMEM((prows, LOCALS * tok_rows), BF16),
            pltpu.VMEM((total, quarter), BF16),
            pltpu.VMEM((total, quarter), BF16),
            pltpu.VMEM((quarter, 2 * ff), BF16),
            pltpu.VMEM((ff, quarter), BF16),
            pltpu.VMEM((total, 2 * ff), BF16),
            pltpu.VMEM((grows, 256), F32),
            pltpu.VMEM((GROUPS, own, 2 * ff), F32),
            pltpu.VMEM((GROUPS, LOCALS - 1, own, 2 * ff), BF16),
            pltpu.VMEM((total, ff), BF16),
            pltpu.VMEM((total, quarter), BF16),
            pltpu.VMEM((LOCALS * tok_rows, prows), BF16),
            pltpu.VMEM((LOCALS * tok_rows, prows), BF16),
            pltpu.VMEM((LOCALS * tok_rows, quarter), F32),
            pltpu.VMEM((LOCALS * tok_rows, quarter), BF16),
            dma((3,)), dma((2,)), dma((3,)), dma((3,)), dma((3,)), dma((3,)), dma((3,)), dma((3,)),
            dma((2, 4)), dma((2, 4)), dma((2, 4)), dma((2, 4)),
            dma((4, 8)), dma((4, 8)),
            dma((GROUPS, 3)), dma((GROUPS, 3)), dma((GROUPS, 3)), dma((GROUPS, 3)),
            dma((4, 8)), dma((4, 8)), dma((3,)), dma((3,)),
        ],
        compiler_params=pltpu.CompilerParams(
            collective_id=0, has_side_effects=True, vmem_limit_bytes=62 * 2**20),
        cost_estimate=pl.CostEstimate(flops=20 * 10**9, bytes_accessed=15 * 10**6, transcendentals=10**6),
    )(meta, tokens, w_gate, w_up, w_down)


def solution(mesh):
    placed = (
        P(("node", "local"), None),
        P(("node", "local"), None),
        P(("node", "local"), None),
        P("node", "local", None),
        P("node", "local", None),
        P("node", None, "local"),
    )
    return jax.shard_map(
        shards, mesh=mesh, in_specs=placed, out_specs=P(("node", "local"), None), check_vma=False
    )
```

```python
import functools

import jax
import jax.numpy as jnp
from jax import lax
from jax.experimental import pallas as pl
from jax.experimental.pallas import tpu as pltpu
from jax.sharding import PartitionSpec as P

MESH = pl.DeviceIdType.MESH
F32 = jnp.float32
BF16 = jnp.bfloat16
NODES, LOCALS = 32, 4
STEPS = ((0, 0), (0, 1), (2, 0), (2, 1), (1, 0), (1, 1), (3, 0), (3, 1))
PLANES = (0, 3, 1, 2)
HALVES = 2
PER = len(STEPS) // HALVES
GROUPS = len(PLANES) * HALVES
PARTS = ((0, 3), (3, 7))


def kernel(tok_rows, quarter, ff, cap,
           set_ref, gw_ref, tok_ref, wg_ref, wu_ref, wd_ref, out_ref,
           meta, zin, pick, sbuf, abuf, wgu, wd, pre, part, ownf, nearf, fbuf, rsbuf, hid, rbuf, uhi, ulo, acc, mbuf,
           w_sem, l_sem, o_sem, ms_sem, mr_sem, ns_sem, nr_sem, xs_sem, xr_sem, zs_sem, zr_sem, os_sem, or_sem,
           ds_sem, dr_sem, ps_sem, pr_sem, hs_sem, hr_sem, as_sem, ar_sem, fs_sem, fr_sem):
    slots = LOCALS * cap
    prows = len(STEPS) * slots
    grows = PER * slots
    own = grows // LOCALS
    fh = ff // 2
    ptok = LOCALS * tok_rows
    node, loc = lax.axis_index("node"), lax.axis_index("local")
    z, y, c = node // 8, (node // 2) % 4, node % 2

    def at_node(dz, dy, dc):
        return (((z + dz) % 4) * 4 + (y + dy) % 4) * 2 + (c + dc) % 2

    def back(r, i):
        dy, dc = STEPS[i]
        return at_node(PLANES[r], 4 - dy, dc)

    def expert(r, i):
        dy, dc = STEPS[i]
        return at_node(4 - PLANES[r], dy, dc)

    def xto(d):
        return (loc + d) % LOCALS

    def rows(ref, start, size):
        return ref.at[pl.ds(pl.multiple_of(start, 16), size)]

    def cols(j):
        return pl.ds(pl.multiple_of(j * quarter, 128), quarter)

    def tile(t, base=0):
        return pl.ds(pl.multiple_of(t * 256 + base, 256), 256)

    def remote(src, dst, ss, rs, n, x):
        return pltpu.make_async_remote_copy(
            src_ref=src, dst_ref=dst, send_sem=ss, recv_sem=rs, device_id=(n, x), device_id_type=MESH)

    barrier = pltpu.get_barrier_semaphore()
    for r in range(len(PLANES)):
        for i in range(len(STEPS)):
            if (r, i) != (0, 0):
                pl.semaphore_signal(barrier, inc=1, device_id=(back(r, i), loc), device_id_type=MESH)
    for d in range(1, LOCALS):
        pl.semaphore_signal(barrier, inc=1, device_id=(node, xto(d)), device_id_type=MESH)
    own_tok = pltpu.make_async_copy(tok_ref.at[:, cols(loc)], rows(zin, loc * tok_rows, tok_rows), l_sem.at[0])
    own_tok.start()
    names = lax.broadcasted_iota(jnp.int32, (NODES, tok_rows), 0)
    member = [jnp.where(names == set_ref[r:r + 1, :], 1.0, 0.0) for r in range(2)]
    row, col = (lax.broadcasted_iota(jnp.int32, (tok_rows, tok_rows), k) for k in range(2))
    before = jnp.dot((member[0] + member[1]).astype(BF16), jnp.where(row < col, 1.0, 0.0).astype(BF16),
                     preferred_element_type=F32)
    for r in range(2):
        slot = jnp.sum(member[r] * before, axis=0, keepdims=True)
        meta[0, loc, r:r + 1, :] = (set_ref[r:r + 1, :] * slots).astype(F32) + slot
    meta[0, loc, 2:4, :] = gw_ref[...]
    pl.semaphore_wait(barrier, NODES - 1 + LOCALS - 1)

    m_copies, n_copies, x_copies, z_copies, o_copies = {}, {}, {}, {}, {}
    for d in (1, 3, 2):
        m_copies[d] = remote(meta.at[0, loc], meta.at[0, loc], ms_sem.at[d - 1], mr_sem.at[d - 1], node, xto(d))
        m_copies[d].start()

    def z_send(d, src):
        at = ((loc + LOCALS - d) % LOCALS) * tok_rows
        for r, dz in ((1, 1), (2, 3)):
            z_copies[r, d] = remote(src, rows(zin, r * ptok + at, tok_rows), zs_sem.at[r - 1, d], zr_sem.at[r - 1, d],
                                    at_node(dz, 0, 0), loc)
            z_copies[r, d].start()

    arrived = set()

    def z_arrive(r, d):
        if (r, d) not in arrived:
            arrived.add((r, d))
            z_copies[r, d].wait_recv()

    def z_forward(d):
        half = tok_rows // 2
        at = ((loc + LOCALS - d) % LOCALS) * tok_rows
        for r, dz, shift in ((1, 1, 0), (2, 3, half)):
            z_arrive(r, d)
            o_copies[r, d] = remote(rows(zin, r * ptok + at + shift, half), rows(zin, 3 * ptok + at + shift, half),
                                    os_sem.at[r - 1, d], or_sem.at[r - 1, d], at_node(dz, 0, 0), loc)
            o_copies[r, d].start()

    for d in (1, 3, 2):
        x_copies[d] = remote(tok_ref.at[:, cols(xto(d))], rows(zin, loc * tok_rows, tok_rows),
                             xs_sem.at[d - 1], xr_sem.at[d - 1], node, xto(d))
        x_copies[d].start()
    z_send(0, tok_ref.at[:, cols(loc)])
    w_copies = [
        pltpu.make_async_copy(ref.at[0, :, pl.ds(k * fh, fh)], wgu.at[:, pl.ds(k * ff + u * fh, fh)], w_sem.at[k, u])
        for k in range(2) for u, ref in enumerate((wg_ref, wu_ref))
    ] + [
        pltpu.make_async_copy(wd_ref.at[0], wd, w_sem.at[2, 0]),
    ]
    for d in (1, 3, 2):
        m_copies[d].wait()
    for r, dz in ((1, 1), (2, 3), (3, 2)):
        n_copies[r] = remote(meta.at[0], meta.at[r], ns_sem.at[r - 1], nr_sem.at[r - 1], at_node(dz, 0, 0), loc)
        n_copies[r].start()
    for w in w_copies:
        w.start()
    for d in (1, 3, 2):
        x_copies[d].wait_recv()
        z_send(d, rows(zin, ((loc + LOCALS - d) % LOCALS) * tok_rows, tok_rows))
    own_tok.wait()

    d_copies, p_copies, h_copies, a_copies = {}, {}, {}, {}
    seen = []

    def plane_send(r):
        if r > 0:
            n_copies[r].wait_recv()
        if r in (1, 2):
            for d in range(LOCALS):
                z_arrive(r, d)
        if r == 3:
            for d in (0, 1, 3, 2):
                o_copies[1, d].wait_recv()
                o_copies[2, d].wait_recv()
        at = lax.broadcasted_iota(jnp.int32, (slots, tok_rows), 0)
        for i in range(len(STEPS)):
            row_id = (at + at_node(0, *STEPS[i]) * slots).astype(F32)
            for b in range(LOCALS):
                d0 = meta[r, b, 0:1, :] + float(b * cap)
                d1 = meta[r, b, 1:2, :] + float(b * cap)
                hit = jnp.where(row_id == d0, 1.0, 0.0) + jnp.where(row_id == d1, 1.0, 0.0)
                pick[i * slots:(i + 1) * slots, b * tok_rows:(b + 1) * tok_rows] = hit.astype(BF16)

        @pl.loop(0, quarter // 256)
        def _(t):
            got = jnp.dot(pick[...], zin[r * ptok:(r + 1) * ptok, tile(t)], preferred_element_type=F32).astype(BF16)
            abuf[r * prows:r * prows + slots, tile(t)] = got[:slots]
            sbuf[r * prows + slots:(r + 1) * prows, tile(t)] = got[slots:]

        for i in range(1, len(STEPS)):
            at = pl.ds(r * prows + i * slots, slots)
            d_copies[r, i] = remote(sbuf.at[at], abuf.at[at], ds_sem.at[r, i], dr_sem.at[r, i],
                                    at_node(0, *STEPS[i]), loc)
            d_copies[r, i].start()

    def members(g):
        return [(g // HALVES, g % HALVES * PER + j) for j in range(PER)]

    def mine(g, d):
        return pl.ds(pl.multiple_of(g * grows + xto(d) * own, 16), own)

    def p_send(g, k, src, dst, d):
        p_copies[g, k] = remote(src, dst, ps_sem.at[g, k], pr_sem.at[g, k], node, xto(d))
        p_copies[g, k].start()

    first, second = pl.ds(0, ff), pl.ds(ff, ff)

    def stage_a(g):
        for r, i in members(g):
            if i > 0:
                d_copies[r, i].wait_recv()
        if "a" not in seen:
            seen.append("a")
            for w in w_copies[:4]:
                w.wait()

        @pl.loop(0, 2 * ff // 256)
        def _(t):
            part[...] = jnp.dot(abuf[g * grows:(g + 1) * grows, :], wgu[:, tile(t)], preferred_element_type=F32)
            pre[g * grows:(g + 1) * grows, tile(t)] = part[...].astype(BF16)
            ownf[g, :, tile(t)] = part[pl.ds(pl.multiple_of(loc * own, 16), own), :]
            near = (loc + 1 + 2 * (t // (ff // 256))) % LOCALS
            nearf[g, :, tile(t)] = part[pl.ds(pl.multiple_of(near * own, 16), own), :]

        p_send(g, 0, pre.at[mine(g, 2), first], fbuf.at[g, 0], 1)
        p_send(g, 1, pre.at[mine(g, 2), second], fbuf.at[g, 1], 3)
        p_send(g, 2, pre.at[mine(g, 1), second], rsbuf.at[g, 0, :, second], 1)
        p_send(g, 3, pre.at[mine(g, 3), first], rsbuf.at[g, 1, :, first], 3)

    def stage_s(g):
        for k, d, at in ((0, 1, first), (1, 3, second)):
            p_copies[g, k].wait_recv()
            pre[mine(g, d), at] = (nearf[g, :, at] + fbuf[g, k].astype(F32)).astype(BF16)
            p_send(g, 4 + k, pre.at[mine(g, d), at], rsbuf.at[g, k, :, at], d)

    def h_send(g, k, ref, d):
        h_copies[g, k] = remote(ref, ref, hs_sem.at[g, k], hr_sem.at[g, k], node, xto(d))
        h_copies[g, k].start()

    def stage_b(g):
        for k in (2, 3, 4, 5):
            p_copies[g, k].wait_recv()

        @pl.loop(0, ff // 256)
        def _(t):
            at_gate = pl.ds(pl.multiple_of(t // 2 * ff + t % 2 * 256, 256), 256)
            at_up = pl.ds(pl.multiple_of(t // 2 * ff + t % 2 * 256 + fh, 256), 256)
            gate, up = ownf[g, :, at_gate], ownf[g, :, at_up]
            for k in range(2):
                gate = gate + rsbuf[g, k, :, at_gate].astype(F32)
                up = up + rsbuf[g, k, :, at_up].astype(F32)
            hid[mine(g, 0), tile(t)] = (gate / (1.0 + jnp.exp(-gate)) * up).astype(BF16)

        h_send(g, 0, hid.at[mine(g, 0)], 1)
        h_send(g, 1, hid.at[mine(g, 0)], 3)

    def stage_w(g):
        h_copies[g, 0].wait_recv()
        h_send(g, 2, hid.at[mine(g, 3), pl.ds(0, fh)], 1)
        h_copies[g, 1].wait_recv()
        h_send(g, 3, hid.at[mine(g, 1), pl.ds(fh, fh)], 3)

    def a_send(g, k, lo, hi):
        for r, i in members(g):
            if (r, i) != (0, 0):
                at = pl.ds(r * prows + i * slots, slots), pl.ds(lo * 256, (hi - lo) * 256)
                a_copies[r, i, k] = remote(abuf.at[at], rbuf.at[at], as_sem.at[k, r, i], ar_sem.at[k, r, i],
                                           back(r, i), loc)
                a_copies[r, i, k].start()

    def stage_c(g):
        h_copies[g, 2].wait_recv()
        h_copies[g, 3].wait_recv()
        if "c" not in seen:
            seen.append("c")
            w_copies[4].wait()

        @pl.loop(0, quarter // 256)
        def _(t):
            got = jnp.dot(hid[g * grows:(g + 1) * grows, :], wd[:, tile(t)],
                          preferred_element_type=F32).astype(BF16)
            if g == 0:
                rbuf[0:slots, tile(t)] = got[:slots]
                abuf[slots:grows, tile(t)] = got[slots:]
            else:
                abuf[g * grows:(g + 1) * grows, tile(t)] = got

        if g < GROUPS - HALVES:
            a_send(g, 0, 0, quarter // 256)
        else:
            a_send(g, 0, *PARTS[0])
        if g == GROUPS - 1:
            for k in range(1, len(PARTS)):
                for h in range(GROUPS - HALVES, GROUPS):
                    a_send(h, k, *PARTS[k])

    def stage_m(r):
        spot = lax.broadcasted_iota(jnp.int32, (tok_rows, prows), 1)
        slot_id = spot + expert(r, 0) * slots
        for i in range(1, len(STEPS)):
            slot_id = jnp.where(spot >= i * slots, spot + (expert(r, i) - i) * slots, slot_id)
        slot_id = slot_id.astype(F32)
        for b in range(LOCALS):
            m = jnp.transpose(meta[0, b])
            d0, d1 = m[:, 0:1] + float(b * cap), m[:, 1:2] + float(b * cap)
            w = jnp.where(slot_id == d0, m[:, 2:3], 0.0) + jnp.where(slot_id == d1, m[:, 3:4], 0.0)
            high = w.astype(BF16)
            uhi[b * tok_rows:(b + 1) * tok_rows, :] = high
            ulo[b * tok_rows:(b + 1) * tok_rows, :] = (w - high.astype(F32)).astype(BF16)
        for k, (lo, hi) in enumerate(PARTS if r == len(PLANES) - 1 else ((0, quarter // 256),)):
            for i in range(len(STEPS)):
                if (r, i) != (0, 0):
                    a_copies[r, i, k].wait_recv()

            @pl.loop(lo, hi)
            def _(t):
                got = rbuf[r * prows:(r + 1) * prows, tile(t)]
                mix = jnp.dot(uhi[...], got, preferred_element_type=F32) + jnp.dot(
                    ulo[...], got, preferred_element_type=F32)
                if "m" in seen:
                    mix = mix + acc[:, tile(t)]
                if r < len(PLANES) - 1:
                    acc[:, tile(t)] = mix
                else:
                    mbuf[:, tile(t)] = mix.astype(BF16)

            if r < len(PLANES) - 1:
                seen.append("m")
            else:
                here = pl.ds(pl.multiple_of(loc * quarter + lo * 256, 256), (hi - lo) * 256)
                for d in (2, 1, 3):
                    at = pl.ds(pl.multiple_of(xto(d) * tok_rows, 16), tok_rows), pl.ds(lo * 256, (hi - lo) * 256)
                    f_copies[k, d] = remote(mbuf.at[at], out_ref.at[:, here], fs_sem.at[k, d - 1], fr_sem.at[k, d - 1],
                                            node, xto(d))
                    f_copies[k, d].start()
                at = pl.ds(pl.multiple_of(loc * tok_rows, 16), tok_rows), pl.ds(lo * 256, (hi - lo) * 256)
                own_out.append(pltpu.make_async_copy(mbuf.at[at], out_ref.at[:, here], o_sem.at[k]))
                own_out[-1].start()

    f_copies, own_out = {}, []
    z_forward(0)
    z_forward(1)
    plane_send(0)
    stage_a(0)
    plane_send(1)
    stage_a(1)
    plane_send(2)
    z_forward(2)
    stage_s(1)
    z_forward(3)
    stage_a(2)
    stage_b(1)
    stage_s(2)
    stage_a(3)
    stage_b(2)
    stage_a(4)
    plane_send(3)
    stage_w(2)
    stage_s(4)
    stage_a(5)
    stage_c(2)
    stage_b(4)
    stage_s(3)
    stage_w(4)
    stage_s(5)
    stage_b(3)
    stage_s(0)
    stage_c(4)
    stage_b(5)
    stage_w(3)
    stage_a(6)
    stage_w(5)
    stage_w(1)
    stage_c(3)
    stage_s(6)
    stage_b(0)
    stage_c(5)
    stage_b(6)
    stage_a(7)
    stage_w(6)
    stage_w(0)
    stage_s(7)
    stage_c(1)
    stage_c(6)
    stage_b(7)
    stage_m(1)
    stage_w(7)
    stage_c(0)
    stage_c(7)
    stage_m(2)
    stage_m(0)
    stage_m(3)
    for sent in (x_copies, n_copies, z_copies, o_copies, d_copies, a_copies, p_copies, h_copies):
        for copy in sent.values():
            copy.wait_send()
    for copy in own_out + list(f_copies.values()):
        copy.wait()


def shards(tokens, node_set, gate_weights, w_gate, w_up, w_down):
    tok_rows, width = tokens.shape
    quarter = width // LOCALS
    ff = w_gate.shape[2]
    routes = node_set.shape[1]
    cap = 3 * tok_rows * routes // (2 * NODES)
    slots = LOCALS * cap
    total = NODES * slots
    prows = len(STEPS) * slots
    grows = PER * slots
    own = grows // LOCALS

    any_spec = pl.BlockSpec(memory_space=pl.ANY)
    dma = pltpu.SemaphoreType.DMA
    return pl.pallas_call(
        functools.partial(kernel, tok_rows, quarter, ff, cap),
        name="routed_experts",
        out_shape=jax.ShapeDtypeStruct((tok_rows, width), BF16),
        in_specs=[pl.BlockSpec(memory_space=pltpu.VMEM)] * 2 + [any_spec] * 4,
        out_specs=any_spec,
        scratch_shapes=[
            pltpu.VMEM((len(PLANES), LOCALS, 8, tok_rows), F32),
            pltpu.VMEM((len(PLANES) * LOCALS * tok_rows, quarter), BF16),
            pltpu.VMEM((prows, LOCALS * tok_rows), BF16),
            pltpu.VMEM((total, quarter), BF16),
            pltpu.VMEM((total, quarter), BF16),
            pltpu.VMEM((quarter, 2 * ff), BF16),
            pltpu.VMEM((ff, quarter), BF16),
            pltpu.VMEM((total, 2 * ff), BF16),
            pltpu.VMEM((grows, 256), F32),
            pltpu.VMEM((GROUPS, own, 2 * ff), F32),
            pltpu.VMEM((GROUPS, own, 2 * ff), F32),
            pltpu.VMEM((GROUPS, 2, own, ff), BF16),
            pltpu.VMEM((GROUPS, 2, own, 2 * ff), BF16),
            pltpu.VMEM((total, ff), BF16),
            pltpu.VMEM((total, quarter), BF16),
            pltpu.VMEM((LOCALS * tok_rows, prows), BF16),
            pltpu.VMEM((LOCALS * tok_rows, prows), BF16),
            pltpu.VMEM((LOCALS * tok_rows, quarter), F32),
            pltpu.VMEM((LOCALS * tok_rows, quarter), BF16),
            dma((3, 2)), dma((1,)), dma((len(PARTS),)),
            dma((3,)), dma((3,)), dma((3,)), dma((3,)), dma((3,)), dma((3,)),
            dma((2, 4)), dma((2, 4)), dma((2, 4)), dma((2, 4)),
            dma((4, 8)), dma((4, 8)),
            dma((GROUPS, 6)), dma((GROUPS, 6)), dma((GROUPS, 4)), dma((GROUPS, 4)),
            dma((len(PARTS), 4, 8)), dma((len(PARTS), 4, 8)), dma((len(PARTS), 3)), dma((len(PARTS), 3)),
        ],
        compiler_params=pltpu.CompilerParams(
            collective_id=0, has_side_effects=True, vmem_limit_bytes=62 * 2**20),
        cost_estimate=pl.CostEstimate(flops=20 * 10**9, bytes_accessed=15 * 10**6, transcendentals=10**6),
    )(node_set.T, gate_weights.T, tokens, w_gate, w_up, w_down)


def solution(mesh):
    placed = (
        P(("node", "local"), None),
        P(("node", "local"), None),
        P(("node", "local"), None),
        P("node", "local", None),
        P("node", "local", None),
        P("node", None, "local"),
    )
    return jax.shard_map(
        shards, mesh=mesh, in_specs=placed, out_specs=P(("node", "local"), None), check_vma=False
    )
```

```python
import functools

import jax
import jax.numpy as jnp
from jax import lax
from jax.experimental import pallas as pl
from jax.experimental.pallas import tpu as pltpu
from jax.sharding import PartitionSpec as P

MESH = pl.DeviceIdType.MESH
F32 = jnp.float32
BF16 = jnp.bfloat16
NODES, LOCALS = 32, 4
STEPS = ((0, 0), (0, 1), (2, 0), (2, 1), (1, 0), (1, 1), (3, 0), (3, 1))
PLANES = (0, 3, 1, 2)
HALVES = 2
PER = len(STEPS) // HALVES
GROUPS = len(PLANES) * HALVES
PARTS = ((0, 2), (2, 4), (4, 7))


def kernel(tok_rows, quarter, ff, cap,
           set_ref, gw_ref, tok_ref, wg_ref, wu_ref, wd_ref, out_ref,
           meta, zin, pick, sbuf, abuf, wgu, wd, pre, part, ownf, nearf, fbuf, rsbuf, hid, rbuf, uhi, ulo, acc, mbuf,
           w_sem, l_sem, o_sem, ms_sem, mr_sem, ns_sem, nr_sem, xs_sem, xr_sem, zs_sem, zr_sem, os_sem, or_sem,
           ds_sem, dr_sem, ps_sem, pr_sem, hs_sem, hr_sem, as_sem, ar_sem, fs_sem, fr_sem):
    slots = LOCALS * cap
    prows = len(STEPS) * slots
    grows = PER * slots
    own = grows // LOCALS
    fh = ff // 2
    ptok = LOCALS * tok_rows
    node, loc = lax.axis_index("node"), lax.axis_index("local")
    z, y, c = node // 8, (node // 2) % 4, node % 2

    def at_node(dz, dy, dc):
        return (((z + dz) % 4) * 4 + (y + dy) % 4) * 2 + (c + dc) % 2

    def back(r, i):
        dy, dc = STEPS[i]
        return at_node(PLANES[r], 4 - dy, dc)

    def expert(r, i):
        dy, dc = STEPS[i]
        return at_node(4 - PLANES[r], dy, dc)

    def xto(d):
        return (loc + d) % LOCALS

    def rows(ref, start, size):
        return ref.at[pl.ds(pl.multiple_of(start, 16), size)]

    def cols(j):
        return pl.ds(pl.multiple_of(j * quarter, 128), quarter)

    def tile(t, base=0):
        return pl.ds(pl.multiple_of(t * 256 + base, 256), 256)

    def remote(src, dst, ss, rs, n, x):
        return pltpu.make_async_remote_copy(
            src_ref=src, dst_ref=dst, send_sem=ss, recv_sem=rs, device_id=(n, x), device_id_type=MESH)

    barrier = pltpu.get_barrier_semaphore()
    for r in range(len(PLANES)):
        for i in range(len(STEPS)):
            if (r, i) != (0, 0):
                pl.semaphore_signal(barrier, inc=1, device_id=(back(r, i), loc), device_id_type=MESH)
    for d in range(1, LOCALS):
        pl.semaphore_signal(barrier, inc=1, device_id=(node, xto(d)), device_id_type=MESH)
    own_tok = pltpu.make_async_copy(tok_ref.at[:, cols(loc)], rows(zin, loc * tok_rows, tok_rows), l_sem.at[0])
    own_tok.start()
    names = lax.broadcasted_iota(jnp.int32, (NODES, tok_rows), 0)
    member = [jnp.where(names == set_ref[r:r + 1, :], 1.0, 0.0) for r in range(2)]
    row, col = (lax.broadcasted_iota(jnp.int32, (tok_rows, tok_rows), k) for k in range(2))
    before = jnp.dot((member[0] + member[1]).astype(BF16), jnp.where(row < col, 1.0, 0.0).astype(BF16),
                     preferred_element_type=F32)
    for r in range(2):
        slot = jnp.sum(member[r] * before, axis=0, keepdims=True)
        meta[0, loc, r:r + 1, :] = (set_ref[r:r + 1, :] * slots).astype(F32) + slot
    meta[0, loc, 2:4, :] = gw_ref[...]
    pl.semaphore_wait(barrier, NODES - 1 + LOCALS - 1)

    m_copies, n_copies, x_copies, z_copies, o_copies = {}, {}, {}, {}, {}
    for d in (1, 3, 2):
        m_copies[d] = remote(meta.at[0, loc], meta.at[0, loc], ms_sem.at[d - 1], mr_sem.at[d - 1], node, xto(d))
        m_copies[d].start()

    def z_send(d, src):
        at = ((loc + LOCALS - d) % LOCALS) * tok_rows
        for r, dz in ((1, 1), (2, 3)):
            z_copies[r, d] = remote(src, rows(zin, r * ptok + at, tok_rows), zs_sem.at[r - 1, d], zr_sem.at[r - 1, d],
                                    at_node(dz, 0, 0), loc)
            z_copies[r, d].start()

    arrived = set()

    def z_arrive(r, d):
        if (r, d) not in arrived:
            arrived.add((r, d))
            z_copies[r, d].wait_recv()

    def z_forward(d):
        half = tok_rows // 2
        at = ((loc + LOCALS - d) % LOCALS) * tok_rows
        for r, dz, shift in ((1, 1, 0), (2, 3, half)):
            z_arrive(r, d)
            o_copies[r, d] = remote(rows(zin, r * ptok + at + shift, half), rows(zin, 3 * ptok + at + shift, half),
                                    os_sem.at[r - 1, d], or_sem.at[r - 1, d], at_node(dz, 0, 0), loc)
            o_copies[r, d].start()

    for d in (1, 3, 2):
        x_copies[d] = remote(tok_ref.at[:, cols(xto(d))], rows(zin, loc * tok_rows, tok_rows),
                             xs_sem.at[d - 1], xr_sem.at[d - 1], node, xto(d))
        x_copies[d].start()
    z_send(0, tok_ref.at[:, cols(loc)])
    w_copies = [
        pltpu.make_async_copy(ref.at[0, :, pl.ds(k * fh, fh)], wgu.at[:, pl.ds(k * ff + u * fh, fh)], w_sem.at[k, u])
        for k in range(2) for u, ref in enumerate((wg_ref, wu_ref))
    ] + [
        pltpu.make_async_copy(wd_ref.at[0], wd, w_sem.at[2, 0]),
    ]
    for d in (1, 3, 2):
        m_copies[d].wait()
    for r, dz in ((1, 1), (2, 3), (3, 2)):
        n_copies[r] = remote(meta.at[0], meta.at[r], ns_sem.at[r - 1], nr_sem.at[r - 1], at_node(dz, 0, 0), loc)
        n_copies[r].start()
    for w in w_copies:
        w.start()
    for d in (1, 3, 2):
        x_copies[d].wait_recv()
        z_send(d, rows(zin, ((loc + LOCALS - d) % LOCALS) * tok_rows, tok_rows))
    own_tok.wait()

    d_copies, p_copies, h_copies, a_copies = {}, {}, {}, {}
    seen = []

    def plane_send(r):
        if r > 0:
            n_copies[r].wait_recv()
        if r in (1, 2):
            for d in range(LOCALS):
                z_arrive(r, d)
        if r == 3:
            for d in (0, 1, 3, 2):
                o_copies[1, d].wait_recv()
                o_copies[2, d].wait_recv()
        at = lax.broadcasted_iota(jnp.int32, (slots, tok_rows), 0)
        for i in range(len(STEPS)):
            row_id = (at + at_node(0, *STEPS[i]) * slots).astype(F32)
            for b in range(LOCALS):
                d0 = meta[r, b, 0:1, :] + float(b * cap)
                d1 = meta[r, b, 1:2, :] + float(b * cap)
                hit = jnp.where(row_id == d0, 1.0, 0.0) + jnp.where(row_id == d1, 1.0, 0.0)
                pick[i * slots:(i + 1) * slots, b * tok_rows:(b + 1) * tok_rows] = hit.astype(BF16)

        @pl.loop(0, quarter // 256)
        def _(t):
            got = jnp.dot(pick[...], zin[r * ptok:(r + 1) * ptok, tile(t)], preferred_element_type=F32).astype(BF16)
            abuf[r * prows:r * prows + slots, tile(t)] = got[:slots]
            sbuf[r * prows + slots:(r + 1) * prows, tile(t)] = got[slots:]

        plane_copies(r, range(1, PER))

    def plane_more(r):
        plane_copies(r, range(PER, len(STEPS)))

    def plane_copies(r, which):
        for i in which:
            at = pl.ds(r * prows + i * slots, slots)
            d_copies[r, i] = remote(sbuf.at[at], abuf.at[at], ds_sem.at[r, i], dr_sem.at[r, i],
                                    at_node(0, *STEPS[i]), loc)
            d_copies[r, i].start()

    def members(g):
        return [(g // HALVES, g % HALVES * PER + j) for j in range(PER)]

    def mine(g, d):
        return pl.ds(pl.multiple_of(g * grows + xto(d) * own, 16), own)

    def p_send(g, k, src, dst, d):
        p_copies[g, k] = remote(src, dst, ps_sem.at[g, k], pr_sem.at[g, k], node, xto(d))
        p_copies[g, k].start()

    first, second = pl.ds(0, ff), pl.ds(ff, ff)

    def stage_a(g):
        for r, i in members(g):
            if i > 0:
                d_copies[r, i].wait_recv()
        if "a" not in seen:
            seen.append("a")
            for w in w_copies[:4]:
                w.wait()

        @pl.loop(0, 2 * ff // 256)
        def _(t):
            part[...] = jnp.dot(abuf[g * grows:(g + 1) * grows, :], wgu[:, tile(t)], preferred_element_type=F32)
            pre[g * grows:(g + 1) * grows, tile(t)] = part[...].astype(BF16)
            ownf[g, :, tile(t)] = part[pl.ds(pl.multiple_of(loc * own, 16), own), :]
            near = (loc + 1 + 2 * (t // (ff // 256))) % LOCALS
            nearf[g, :, tile(t)] = part[pl.ds(pl.multiple_of(near * own, 16), own), :]

        p_send(g, 0, pre.at[mine(g, 2), first], fbuf.at[g, 0], 1)
        p_send(g, 1, pre.at[mine(g, 2), second], fbuf.at[g, 1], 3)

    def stage_s(g):
        for k, d, at in ((0, 1, first), (1, 3, second)):
            p_copies[g, k].wait_recv()
            pre[mine(g, d), at] = (nearf[g, :, at] + fbuf[g, k].astype(F32)).astype(BF16)
            p_send(g, 2 + k, pre.at[mine(g, d)], rsbuf.at[g, k], d)

    def h_send(g, k, ref, d):
        h_copies[g, k] = remote(ref, ref, hs_sem.at[g, k], hr_sem.at[g, k], node, xto(d))
        h_copies[g, k].start()

    def stage_b(g):
        for k in (2, 3):
            p_copies[g, k].wait_recv()

        @pl.loop(0, ff // 256)
        def _(t):
            at_gate = pl.ds(pl.multiple_of(t // 2 * ff + t % 2 * 256, 256), 256)
            at_up = pl.ds(pl.multiple_of(t // 2 * ff + t % 2 * 256 + fh, 256), 256)
            gate, up = ownf[g, :, at_gate], ownf[g, :, at_up]
            for k in range(2):
                gate = gate + rsbuf[g, k, :, at_gate].astype(F32)
                up = up + rsbuf[g, k, :, at_up].astype(F32)
            hid[mine(g, 0), tile(t)] = (gate / (1.0 + jnp.exp(-gate)) * up).astype(BF16)

        h_send(g, 0, hid.at[mine(g, 0)], 1)
        h_send(g, 1, hid.at[mine(g, 0)], 3)

    def stage_w(g):
        h_copies[g, 0].wait_recv()
        h_send(g, 2, hid.at[mine(g, 3), pl.ds(0, fh)], 1)
        h_copies[g, 1].wait_recv()
        h_send(g, 3, hid.at[mine(g, 1), pl.ds(fh, fh)], 3)

    def a_send(g, k, lo, hi):
        for r, i in members(g):
            if (r, i) != (0, 0):
                at = pl.ds(r * prows + i * slots, slots), pl.ds(lo * 256, (hi - lo) * 256)
                a_copies[r, i, k] = remote(abuf.at[at], rbuf.at[at], as_sem.at[k, r, i], ar_sem.at[k, r, i],
                                           back(r, i), loc)
                a_copies[r, i, k].start()

    def stage_c(g):
        h_copies[g, 2].wait_recv()
        h_copies[g, 3].wait_recv()
        if "c" not in seen:
            seen.append("c")
            w_copies[4].wait()

        @pl.loop(0, quarter // 256)
        def _(t):
            got = jnp.dot(hid[g * grows:(g + 1) * grows, :], wd[:, tile(t)],
                          preferred_element_type=F32).astype(BF16)
            if g == 0:
                rbuf[0:slots, tile(t)] = got[:slots]
                abuf[slots:grows, tile(t)] = got[slots:]
            else:
                abuf[g * grows:(g + 1) * grows, tile(t)] = got

        if g < GROUPS - HALVES:
            a_send(g, 0, 0, quarter // 256)
        else:
            a_send(g, 0, *PARTS[0])

    left = set()

    def last_parts(k):
        if k >= 9:
            for r, i in members(GROUPS - 2) + members(GROUPS - 1):
                a_copies[r, i, k - 2].wait_send()
                left.add((r, i, k - 2))
        for h in range(GROUPS - HALVES, GROUPS):
            a_send(h, k, *PARTS[k])

    def stage_m(r):
        spot = lax.broadcasted_iota(jnp.int32, (tok_rows, prows), 1)
        slot_id = spot + expert(r, 0) * slots
        for i in range(1, len(STEPS)):
            slot_id = jnp.where(spot >= i * slots, spot + (expert(r, i) - i) * slots, slot_id)
        slot_id = slot_id.astype(F32)
        for b in range(LOCALS):
            m = jnp.transpose(meta[0, b])
            d0, d1 = m[:, 0:1] + float(b * cap), m[:, 1:2] + float(b * cap)
            w = jnp.where(slot_id == d0, m[:, 2:3], 0.0) + jnp.where(slot_id == d1, m[:, 3:4], 0.0)
            high = w.astype(BF16)
            uhi[b * tok_rows:(b + 1) * tok_rows, :] = high
            ulo[b * tok_rows:(b + 1) * tok_rows, :] = (w - high.astype(F32)).astype(BF16)
        for k, (lo, hi) in enumerate(PARTS if r == len(PLANES) - 1 else ((0, quarter // 256),)):
            for i in range(len(STEPS)):
                if (r, i) != (0, 0):
                    a_copies[r, i, k].wait_recv()

            @pl.loop(lo, hi)
            def _(t):
                got = rbuf[r * prows:(r + 1) * prows, tile(t)]
                mix = jnp.dot(uhi[...], got, preferred_element_type=F32) + jnp.dot(
                    ulo[...], got, preferred_element_type=F32)
                if "m" in seen:
                    mix = mix + acc[:, tile(t)]
                if r < len(PLANES) - 1:
                    acc[:, tile(t)] = mix
                else:
                    mbuf[:, tile(t)] = mix.astype(BF16)

            if r < len(PLANES) - 1:
                seen.append("m")
            else:
                here = pl.ds(pl.multiple_of(loc * quarter + lo * 256, 256), (hi - lo) * 256)
                for d in (2, 1, 3):
                    at = pl.ds(pl.multiple_of(xto(d) * tok_rows, 16), tok_rows), pl.ds(lo * 256, (hi - lo) * 256)
                    f_copies[k, d] = remote(mbuf.at[at], out_ref.at[:, here], fs_sem.at[k, d - 1], fr_sem.at[k, d - 1],
                                            node, xto(d))
                    f_copies[k, d].start()
                at = pl.ds(pl.multiple_of(loc * tok_rows, 16), tok_rows), pl.ds(lo * 256, (hi - lo) * 256)
                own_out.append(pltpu.make_async_copy(mbuf.at[at], out_ref.at[:, here], o_sem.at[k]))
                own_out[-1].start()

    f_copies, own_out = {}, []
    z_forward(0)
    z_forward(1)
    plane_send(0)
    plane_more(0)
    stage_a(0)
    plane_send(1)
    plane_more(1)
    stage_a(1)
    plane_send(2)
    plane_more(2)
    z_forward(2)
    stage_s(1)
    z_forward(3)
    stage_a(2)
    stage_b(1)
    stage_s(2)
    stage_a(3)
    stage_b(2)
    stage_a(4)
    plane_send(3)
    plane_more(3)
    stage_w(2)
    stage_s(4)
    stage_a(5)
    stage_c(2)
    stage_b(4)
    stage_s(3)
    stage_w(4)
    stage_s(5)
    stage_b(3)
    stage_s(0)
    stage_c(4)
    stage_b(5)
    stage_w(3)
    stage_a(6)
    stage_w(5)
    stage_w(1)
    stage_c(3)
    stage_s(6)
    stage_b(0)
    stage_c(5)
    stage_b(6)
    stage_a(7)
    stage_w(6)
    stage_w(0)
    stage_s(7)
    stage_c(1)
    stage_c(6)
    stage_b(7)
    stage_m(1)
    stage_w(7)
    stage_c(0)
    stage_c(7)
    last_parts(1)
    last_parts(2)
    stage_m(2)
    stage_m(0)
    stage_m(3)
    for sent in (x_copies, n_copies, z_copies, o_copies, d_copies, p_copies, h_copies):
        for copy in sent.values():
            copy.wait_send()
    for key, copy in a_copies.items():
        if key not in left:
            copy.wait_send()
    for copy in own_out + list(f_copies.values()):
        copy.wait()


def shards(tokens, node_set, gate_weights, w_gate, w_up, w_down):
    tok_rows, width = tokens.shape
    quarter = width // LOCALS
    ff = w_gate.shape[2]
    routes = node_set.shape[1]
    cap = 3 * tok_rows * routes // (2 * NODES)
    slots = LOCALS * cap
    total = NODES * slots
    prows = len(STEPS) * slots
    grows = PER * slots
    own = grows // LOCALS

    any_spec = pl.BlockSpec(memory_space=pl.ANY)
    dma = pltpu.SemaphoreType.DMA
    return pl.pallas_call(
        functools.partial(kernel, tok_rows, quarter, ff, cap),
        name="routed_experts",
        out_shape=jax.ShapeDtypeStruct((tok_rows, width), BF16),
        in_specs=[pl.BlockSpec(memory_space=pltpu.VMEM)] * 2 + [any_spec] * 4,
        out_specs=any_spec,
        scratch_shapes=[
            pltpu.VMEM((len(PLANES), LOCALS, 8, tok_rows), F32),
            pltpu.VMEM((len(PLANES) * LOCALS * tok_rows, quarter), BF16),
            pltpu.VMEM((prows, LOCALS * tok_rows), BF16),
            pltpu.VMEM((total, quarter), BF16),
            pltpu.VMEM((total, quarter), BF16),
            pltpu.VMEM((quarter, 2 * ff), BF16),
            pltpu.VMEM((ff, quarter), BF16),
            pltpu.VMEM((total, 2 * ff), BF16),
            pltpu.VMEM((grows, 256), F32),
            pltpu.VMEM((GROUPS, own, 2 * ff), F32),
            pltpu.VMEM((GROUPS, own, 2 * ff), F32),
            pltpu.VMEM((GROUPS, 2, own, ff), BF16),
            pltpu.VMEM((GROUPS, 2, own, 2 * ff), BF16),
            pltpu.VMEM((total, ff), BF16),
            pltpu.VMEM((total, quarter), BF16),
            pltpu.VMEM((LOCALS * tok_rows, prows), BF16),
            pltpu.VMEM((LOCALS * tok_rows, prows), BF16),
            pltpu.VMEM((LOCALS * tok_rows, quarter), F32),
            pltpu.VMEM((LOCALS * tok_rows, quarter), BF16),
            dma((3, 2)), dma((1,)), dma((len(PARTS),)),
            dma((3,)), dma((3,)), dma((3,)), dma((3,)), dma((3,)), dma((3,)),
            dma((2, 4)), dma((2, 4)), dma((2, 4)), dma((2, 4)),
            dma((4, 8)), dma((4, 8)),
            dma((GROUPS, 4)), dma((GROUPS, 4)), dma((GROUPS, 4)), dma((GROUPS, 4)),
            dma((len(PARTS), 4, 8)), dma((len(PARTS), 4, 8)), dma((len(PARTS), 3)), dma((len(PARTS), 3)),
        ],
        compiler_params=pltpu.CompilerParams(
            collective_id=0, has_side_effects=True, vmem_limit_bytes=62 * 2**20),
        cost_estimate=pl.CostEstimate(flops=20 * 10**9, bytes_accessed=15 * 10**6, transcendentals=10**6),
    )(node_set.T, gate_weights.T, tokens, w_gate, w_up, w_down)


def solution(mesh):
    placed = (
        P(("node", "local"), None),
        P(("node", "local"), None),
        P(("node", "local"), None),
        P("node", "local", None),
        P("node", "local", None),
        P("node", None, "local"),
    )
    return jax.shard_map(
        shards, mesh=mesh, in_specs=placed, out_specs=P(("node", "local"), None), check_vma=False
    )
```

```python
import functools

import jax
import jax.numpy as jnp
from jax import lax
from jax.experimental import pallas as pl
from jax.experimental.pallas import tpu as pltpu
from jax.sharding import PartitionSpec as P

MESH = pl.DeviceIdType.MESH
F32 = jnp.float32
BF16 = jnp.bfloat16
NODES, LOCALS = 32, 4
STEPS = ((0, 0), (0, 1), (2, 0), (2, 1), (1, 0), (1, 1), (3, 0), (3, 1))
PLANES = (0, 3, 1, 2)
HALVES = 2
PER = len(STEPS) // HALVES
GROUPS = len(PLANES) * HALVES
PARTS = ((0, 2), (2, 4), (4, 7))


def kernel(tok_rows, quarter, ff, cap,
           set_ref, gw_ref, tok_ref, wg_ref, wu_ref, wd_ref, out_ref,
           meta, zin, pick, sbuf, abuf, wgu, wd, pre, part, ownf, nearf, fbuf, rsbuf, hid, rbuf, uhi, ulo, acc, mbuf,
           w_sem, l_sem, o_sem, ms_sem, mr_sem, ns_sem, nr_sem, xs_sem, xr_sem, zs_sem, zr_sem, os_sem, or_sem,
           ds_sem, dr_sem, ps_sem, pr_sem, hs_sem, hr_sem, as_sem, ar_sem, fs_sem, fr_sem):
    slots = LOCALS * cap
    prows = len(STEPS) * slots
    grows = PER * slots
    own = grows // LOCALS
    fh = ff // 2
    ptok = LOCALS * tok_rows
    node, loc = lax.axis_index("node"), lax.axis_index("local")
    z, y, c = node // 8, (node // 2) % 4, node % 2

    def at_node(dz, dy, dc):
        return (((z + dz) % 4) * 4 + (y + dy) % 4) * 2 + (c + dc) % 2

    def back(r, i):
        dy, dc = STEPS[i]
        return at_node(PLANES[r], 4 - dy, dc)

    def expert(r, i):
        dy, dc = STEPS[i]
        return at_node(4 - PLANES[r], dy, dc)

    def xto(d):
        return (loc + d) % LOCALS

    def rows(ref, start, size):
        return ref.at[pl.ds(pl.multiple_of(start, 16), size)]

    def cols(j):
        return pl.ds(pl.multiple_of(j * quarter, 128), quarter)

    def tile(t, base=0):
        return pl.ds(pl.multiple_of(t * 256 + base, 256), 256)

    def remote(src, dst, ss, rs, n, x):
        return pltpu.make_async_remote_copy(
            src_ref=src, dst_ref=dst, send_sem=ss, recv_sem=rs, device_id=(n, x), device_id_type=MESH)

    barrier = pltpu.get_barrier_semaphore()
    for r in range(len(PLANES)):
        for i in range(len(STEPS)):
            if (r, i) != (0, 0):
                pl.semaphore_signal(barrier, inc=1, device_id=(back(r, i), loc), device_id_type=MESH)
    for d in range(1, LOCALS):
        pl.semaphore_signal(barrier, inc=1, device_id=(node, xto(d)), device_id_type=MESH)
    own_tok = pltpu.make_async_copy(tok_ref.at[:, cols(loc)], rows(zin, loc * tok_rows, tok_rows), l_sem.at[0])
    own_tok.start()
    names = lax.broadcasted_iota(jnp.int32, (NODES, tok_rows), 0)
    member = [jnp.where(names == set_ref[r:r + 1, :], 1.0, 0.0) for r in range(2)]
    row, col = (lax.broadcasted_iota(jnp.int32, (tok_rows, tok_rows), k) for k in range(2))
    before = jnp.dot((member[0] + member[1]).astype(BF16), jnp.where(row < col, 1.0, 0.0).astype(BF16),
                     preferred_element_type=F32)
    for r in range(2):
        slot = jnp.sum(member[r] * before, axis=0, keepdims=True)
        meta[0, loc, r:r + 1, :] = (set_ref[r:r + 1, :] * slots).astype(F32) + slot
    meta[0, loc, 2:4, :] = gw_ref[...]
    pl.semaphore_wait(barrier, NODES - 1 + LOCALS - 1)

    m_copies, n_copies, x_copies, z_copies, o_copies = {}, {}, {}, {}, {}
    for d in (1, 3, 2):
        m_copies[d] = remote(meta.at[0, loc], meta.at[0, loc], ms_sem.at[d - 1], mr_sem.at[d - 1], node, xto(d))
        m_copies[d].start()

    def z_send(d, src):
        at = ((loc + LOCALS - d) % LOCALS) * tok_rows
        for r, dz in ((1, 1), (2, 3)):
            z_copies[r, d] = remote(src, rows(zin, r * ptok + at, tok_rows), zs_sem.at[r - 1, d], zr_sem.at[r - 1, d],
                                    at_node(dz, 0, 0), loc)
            z_copies[r, d].start()

    arrived = set()

    def z_arrive(r, d):
        if (r, d) not in arrived:
            arrived.add((r, d))
            z_copies[r, d].wait_recv()

    def z_forward(d):
        half = tok_rows // 2
        at = ((loc + LOCALS - d) % LOCALS) * tok_rows
        for r, dz, shift in ((1, 1, 0), (2, 3, half)):
            z_arrive(r, d)
            o_copies[r, d] = remote(rows(zin, r * ptok + at + shift, half), rows(zin, 3 * ptok + at + shift, half),
                                    os_sem.at[r - 1, d], or_sem.at[r - 1, d], at_node(dz, 0, 0), loc)
            o_copies[r, d].start()

    for d in (1, 3, 2):
        x_copies[d] = remote(tok_ref.at[:, cols(xto(d))], rows(zin, loc * tok_rows, tok_rows),
                             xs_sem.at[d - 1], xr_sem.at[d - 1], node, xto(d))
        x_copies[d].start()
    z_send(0, tok_ref.at[:, cols(loc)])
    w_copies = [
        pltpu.make_async_copy(ref.at[0, :, pl.ds(k * fh, fh)], wgu.at[:, pl.ds(k * ff + u * fh, fh)], w_sem.at[k, u])
        for k in range(2) for u, ref in enumerate((wg_ref, wu_ref))
    ] + [
        pltpu.make_async_copy(wd_ref.at[0], wd, w_sem.at[2, 0]),
    ]
    for d in (1, 3, 2):
        m_copies[d].wait()
    for r, dz in ((1, 1), (2, 3), (3, 2)):
        n_copies[r] = remote(meta.at[0], meta.at[r], ns_sem.at[r - 1], nr_sem.at[r - 1], at_node(dz, 0, 0), loc)
        n_copies[r].start()
    for w in w_copies:
        w.start()
    for d in (1, 3, 2):
        x_copies[d].wait_recv()
        z_send(d, rows(zin, ((loc + LOCALS - d) % LOCALS) * tok_rows, tok_rows))
    own_tok.wait()

    d_copies, p_copies, h_copies, a_copies = {}, {}, {}, {}
    seen = []

    def plane_send(r):
        if r > 0:
            n_copies[r].wait_recv()
        if r in (1, 2):
            for d in range(LOCALS):
                z_arrive(r, d)
        if r == 3:
            for d in (0, 1, 3, 2):
                o_copies[1, d].wait_recv()
                o_copies[2, d].wait_recv()
        at = lax.broadcasted_iota(jnp.int32, (slots, tok_rows), 0)
        for i in range(len(STEPS)):
            row_id = (at + at_node(0, *STEPS[i]) * slots).astype(F32)
            for b in range(LOCALS):
                d0 = meta[r, b, 0:1, :] + float(b * cap)
                d1 = meta[r, b, 1:2, :] + float(b * cap)
                hit = jnp.where(row_id == d0, 1.0, 0.0) + jnp.where(row_id == d1, 1.0, 0.0)
                pick[i * slots:(i + 1) * slots, b * tok_rows:(b + 1) * tok_rows] = hit.astype(BF16)

        @pl.loop(0, quarter // 256)
        def _(t):
            got = jnp.dot(pick[...], zin[r * ptok:(r + 1) * ptok, tile(t)], preferred_element_type=F32).astype(BF16)
            abuf[r * prows:r * prows + slots, tile(t)] = got[:slots]
            sbuf[r * prows + slots:(r + 1) * prows, tile(t)] = got[slots:]

        plane_copies(r, range(1, PER))

    def plane_more(r):
        plane_copies(r, range(PER, len(STEPS)))

    def plane_copies(r, which):
        for i in which:
            at = pl.ds(r * prows + i * slots, slots)
            d_copies[r, i] = remote(sbuf.at[at], abuf.at[at], ds_sem.at[r, i], dr_sem.at[r, i],
                                    at_node(0, *STEPS[i]), loc)
            d_copies[r, i].start()

    def members(g):
        return [(g // HALVES, g % HALVES * PER + j) for j in range(PER)]

    def mine(g, d):
        return pl.ds(pl.multiple_of(g * grows + xto(d) * own, 16), own)

    def p_send(g, k, src, dst, d):
        p_copies[g, k] = remote(src, dst, ps_sem.at[g, k], pr_sem.at[g, k], node, xto(d))
        p_copies[g, k].start()

    first, second = pl.ds(0, ff), pl.ds(ff, ff)

    def stage_a(g):
        for r, i in members(g):
            if i > 0:
                d_copies[r, i].wait_recv()
        if "a" not in seen:
            seen.append("a")
            for w in w_copies[:4]:
                w.wait()

        @pl.loop(0, 2 * ff // 256)
        def _(t):
            part[...] = jnp.dot(abuf[g * grows:(g + 1) * grows, :], wgu[:, tile(t)], preferred_element_type=F32)
            pre[g * grows:(g + 1) * grows, tile(t)] = part[...].astype(BF16)
            ownf[g, :, tile(t)] = part[pl.ds(pl.multiple_of(loc * own, 16), own), :]
            near = (loc + 1 + 2 * (t // (ff // 256))) % LOCALS
            nearf[g, :, tile(t)] = part[pl.ds(pl.multiple_of(near * own, 16), own), :]

        p_send(g, 0, pre.at[mine(g, 2), first], fbuf.at[g, 0], 1)
        p_send(g, 1, pre.at[mine(g, 2), second], fbuf.at[g, 1], 3)

    def stage_s(g):
        for k, d, at in ((0, 1, first), (1, 3, second)):
            p_copies[g, k].wait_recv()
            pre[mine(g, d), at] = (nearf[g, :, at] + fbuf[g, k].astype(F32)).astype(BF16)
            p_send(g, 2 + k, pre.at[mine(g, d)], rsbuf.at[g, k], d)

    def h_send(g, k, ref, d):
        h_copies[g, k] = remote(ref, ref, hs_sem.at[g, k], hr_sem.at[g, k], node, xto(d))
        h_copies[g, k].start()

    def stage_b(g):
        for k in (2, 3):
            p_copies[g, k].wait_recv()

        @pl.loop(0, ff // 256)
        def _(t):
            at_gate = pl.ds(pl.multiple_of(t // 2 * ff + t % 2 * 256, 256), 256)
            at_up = pl.ds(pl.multiple_of(t // 2 * ff + t % 2 * 256 + fh, 256), 256)
            gate, up = ownf[g, :, at_gate], ownf[g, :, at_up]
            for k in range(2):
                gate = gate + rsbuf[g, k, :, at_gate].astype(F32)
                up = up + rsbuf[g, k, :, at_up].astype(F32)
            hid[mine(g, 0), tile(t)] = (gate / (1.0 + jnp.exp(-gate)) * up).astype(BF16)

        h_send(g, 0, hid.at[mine(g, 0)], 1)
        h_send(g, 1, hid.at[mine(g, 0)], 3)

    def stage_w(g):
        h_copies[g, 0].wait_recv()
        h_send(g, 2, hid.at[mine(g, 3), pl.ds(0, fh)], 1)
        h_copies[g, 1].wait_recv()
        h_send(g, 3, hid.at[mine(g, 1), pl.ds(fh, fh)], 3)

    def a_send(g, k, lo, hi):
        for r, i in members(g):
            if (r, i) != (0, 0):
                at = pl.ds(r * prows + i * slots, slots), pl.ds(lo * 256, (hi - lo) * 256)
                a_copies[r, i, k] = remote(abuf.at[at], rbuf.at[at], as_sem.at[k, r, i], ar_sem.at[k, r, i],
                                           back(r, i), loc)
                a_copies[r, i, k].start()

    def stage_c(g):
        h_copies[g, 2].wait_recv()
        h_copies[g, 3].wait_recv()
        if "c" not in seen:
            seen.append("c")
            w_copies[4].wait()

        @pl.loop(0, quarter // 256)
        def _(t):
            got = jnp.dot(hid[g * grows:(g + 1) * grows, :], wd[:, tile(t)],
                          preferred_element_type=F32).astype(BF16)
            if g == 0:
                rbuf[0:slots, tile(t)] = got[:slots]
                abuf[slots:grows, tile(t)] = got[slots:]
            else:
                abuf[g * grows:(g + 1) * grows, tile(t)] = got

        if g < GROUPS - HALVES:
            a_send(g, 0, 0, quarter // 256)
        else:
            a_send(g, 0, *PARTS[0])

    left = set()

    def last_parts(k):
        if k >= 9:
            for r, i in members(GROUPS - 2) + members(GROUPS - 1):
                a_copies[r, i, k - 2].wait_send()
                left.add((r, i, k - 2))
        for h in range(GROUPS - HALVES, GROUPS):
            a_send(h, k, *PARTS[k])

    def stage_m(r):
        spot = lax.broadcasted_iota(jnp.int32, (tok_rows, prows), 1)
        slot_id = spot + expert(r, 0) * slots
        for i in range(1, len(STEPS)):
            slot_id = jnp.where(spot >= i * slots, spot + (expert(r, i) - i) * slots, slot_id)
        slot_id = slot_id.astype(F32)
        for b in range(LOCALS):
            m = jnp.transpose(meta[0, b])
            d0, d1 = m[:, 0:1] + float(b * cap), m[:, 1:2] + float(b * cap)
            w = jnp.where(slot_id == d0, m[:, 2:3], 0.0) + jnp.where(slot_id == d1, m[:, 3:4], 0.0)
            high = w.astype(BF16)
            uhi[b * tok_rows:(b + 1) * tok_rows, :] = high
            ulo[b * tok_rows:(b + 1) * tok_rows, :] = (w - high.astype(F32)).astype(BF16)
        for k, (lo, hi) in enumerate(PARTS if r == len(PLANES) - 1 else ((0, quarter // 256),)):
            for i in range(len(STEPS)):
                if (r, i) != (0, 0):
                    a_copies[r, i, k].wait_recv()

            @pl.loop(lo, hi)
            def _(t):
                got = rbuf[r * prows:(r + 1) * prows, tile(t)]
                mix = jnp.dot(uhi[...], got, preferred_element_type=F32) + jnp.dot(
                    ulo[...], got, preferred_element_type=F32)
                if "m" in seen:
                    mix = mix + acc[:, tile(t)]
                if r < len(PLANES) - 1:
                    acc[:, tile(t)] = mix
                else:
                    mbuf[:, tile(t)] = mix.astype(BF16)

            if r < len(PLANES) - 1:
                seen.append("m")
            else:
                here = pl.ds(pl.multiple_of(loc * quarter + lo * 256, 256), (hi - lo) * 256)
                for d in (2, 1, 3):
                    at = pl.ds(pl.multiple_of(xto(d) * tok_rows, 16), tok_rows), pl.ds(lo * 256, (hi - lo) * 256)
                    f_copies[k, d] = remote(mbuf.at[at], out_ref.at[:, here], fs_sem.at[k, d - 1], fr_sem.at[k, d - 1],
                                            node, xto(d))
                    f_copies[k, d].start()
                at = pl.ds(pl.multiple_of(loc * tok_rows, 16), tok_rows), pl.ds(lo * 256, (hi - lo) * 256)
                own_out.append(pltpu.make_async_copy(mbuf.at[at], out_ref.at[:, here], o_sem.at[k]))
                own_out[-1].start()

    f_copies, own_out = {}, []
    z_forward(0)
    z_forward(1)
    plane_send(0)
    plane_more(0)
    stage_a(0)
    plane_send(1)
    plane_more(1)
    stage_a(1)
    stage_s(0)
    plane_send(2)
    plane_more(2)
    z_forward(2)
    stage_s(1)
    z_forward(3)
    stage_a(2)
    stage_b(0)
    stage_b(1)
    stage_s(2)
    stage_a(3)
    stage_b(2)
    stage_a(4)
    plane_send(3)
    plane_more(3)
    stage_w(0)
    stage_w(2)
    stage_s(4)
    stage_a(5)
    stage_c(2)
    stage_b(4)
    stage_s(3)
    stage_w(4)
    stage_s(5)
    stage_b(3)
    stage_c(4)
    stage_b(5)
    stage_w(3)
    stage_a(6)
    stage_w(5)
    stage_w(1)
    stage_c(3)
    stage_s(6)
    stage_c(5)
    stage_b(6)
    stage_a(7)
    stage_w(6)
    stage_s(7)
    stage_c(1)
    stage_c(6)
    stage_b(7)
    stage_c(0)
    stage_w(7)
    stage_c(7)
    last_parts(1)
    last_parts(2)
    stage_m(1)
    stage_m(2)
    stage_m(0)
    stage_m(3)
    for sent in (x_copies, n_copies, z_copies, o_copies, d_copies, p_copies, h_copies):
        for copy in sent.values():
            copy.wait_send()
    for key, copy in a_copies.items():
        if key not in left:
            copy.wait_send()
    for copy in own_out + list(f_copies.values()):
        copy.wait()


def shards(tokens, node_set, gate_weights, w_gate, w_up, w_down):
    tok_rows, width = tokens.shape
    quarter = width // LOCALS
    ff = w_gate.shape[2]
    routes = node_set.shape[1]
    cap = 3 * tok_rows * routes // (2 * NODES)
    slots = LOCALS * cap
    total = NODES * slots
    prows = len(STEPS) * slots
    grows = PER * slots
    own = grows // LOCALS

    any_spec = pl.BlockSpec(memory_space=pl.ANY)
    dma = pltpu.SemaphoreType.DMA
    return pl.pallas_call(
        functools.partial(kernel, tok_rows, quarter, ff, cap),
        name="routed_experts",
        out_shape=jax.ShapeDtypeStruct((tok_rows, width), BF16),
        in_specs=[pl.BlockSpec(memory_space=pltpu.VMEM)] * 2 + [any_spec] * 4,
        out_specs=any_spec,
        scratch_shapes=[
            pltpu.VMEM((len(PLANES), LOCALS, 8, tok_rows), F32),
            pltpu.VMEM((len(PLANES) * LOCALS * tok_rows, quarter), BF16),
            pltpu.VMEM((prows, LOCALS * tok_rows), BF16),
            pltpu.VMEM((total, quarter), BF16),
            pltpu.VMEM((total, quarter), BF16),
            pltpu.VMEM((quarter, 2 * ff), BF16),
            pltpu.VMEM((ff, quarter), BF16),
            pltpu.VMEM((total, 2 * ff), BF16),
            pltpu.VMEM((grows, 256), F32),
            pltpu.VMEM((GROUPS, own, 2 * ff), F32),
            pltpu.VMEM((GROUPS, own, 2 * ff), F32),
            pltpu.VMEM((GROUPS, 2, own, ff), BF16),
            pltpu.VMEM((GROUPS, 2, own, 2 * ff), BF16),
            pltpu.VMEM((total, ff), BF16),
            pltpu.VMEM((total, quarter), BF16),
            pltpu.VMEM((LOCALS * tok_rows, prows), BF16),
            pltpu.VMEM((LOCALS * tok_rows, prows), BF16),
            pltpu.VMEM((LOCALS * tok_rows, quarter), F32),
            pltpu.VMEM((LOCALS * tok_rows, quarter), BF16),
            dma((3, 2)), dma((1,)), dma((len(PARTS),)),
            dma((3,)), dma((3,)), dma((3,)), dma((3,)), dma((3,)), dma((3,)),
            dma((2, 4)), dma((2, 4)), dma((2, 4)), dma((2, 4)),
            dma((4, 8)), dma((4, 8)),
            dma((GROUPS, 4)), dma((GROUPS, 4)), dma((GROUPS, 4)), dma((GROUPS, 4)),
            dma((len(PARTS), 4, 8)), dma((len(PARTS), 4, 8)), dma((len(PARTS), 3)), dma((len(PARTS), 3)),
        ],
        compiler_params=pltpu.CompilerParams(
            collective_id=0, has_side_effects=True, vmem_limit_bytes=62 * 2**20),
        cost_estimate=pl.CostEstimate(flops=20 * 10**9, bytes_accessed=15 * 10**6, transcendentals=10**6),
    )(node_set.T, gate_weights.T, tokens, w_gate, w_up, w_down)


def solution(mesh):
    placed = (
        P(("node", "local"), None),
        P(("node", "local"), None),
        P(("node", "local"), None),
        P("node", "local", None),
        P("node", "local", None),
        P("node", None, "local"),
    )
    return jax.shard_map(
        shards, mesh=mesh, in_specs=placed, out_specs=P(("node", "local"), None), check_vma=False
    )
```
